256 devices in a mesh: seq: 8 (over y, z_lo), head: 32 (over x, z_hi, core).
Axes of the slice: x: 4, y: 4, z: 8 (z_hi: 4, z_lo: 2; z = z_hi * 2 + z_lo), core: 2. Of those that a mesh axis runs over, the one named last changes fastest.
Arguments:
- queries: bfloat16 [2048, 128, 576], P('seq', 'head'), may hold values from -200 to 200
- latent_cache: bfloat16 [2048, 576], P('seq'), may hold values from -6 to 6
- grad_output: bfloat16 [2048, 128, 512], P('seq', 'head'), may hold values from -6 to 6
- query_blocks: int32 [8], replicated, may hold values from 0 to 127, as said below
- key_blocks: int32 [8], replicated, may hold values from 0 to 127, as said below
Outputs:
- grad_queries: bfloat16 [2048, 128, 576], P('seq', 'head')
- grad_cache: float32 [2048, 576], P(('seq', 'head'))
The draws below stay inside these ranges and needn't reach their ends.
Inputs may be any that keep to these rules, and one draw needn't show every extreme that they name: `query_blocks`: the groups hold distinct block positions, one of them 16 * 8 - 1. `key_blocks`: the groups hold distinct block positions, one of them 0 and one 16 * 8 - 1.
All inputs are finite; a program needn't handle non-finite values.
Results may differ from the reference program's by a relative error of at most 0.013.
Values may be sent and summed in bfloat16 or wider, within the bound.
No kernel may reach another device: no remote copies, remote signals or barrier semaphores. Data moves between devices by JAX's collectives and lax.ppermute only.
A program may use at most 64 MiB of HBM per device.

```python
import jax
import jax.numpy as jnp
from jax import lax

H = 128
DL = 512
DR = 64
TILE = 256
DK = 576
SEQLEN = 2048
N_SEQ = 8


def shared_orders(key):
    span = 16 * N_SEQ
    query_rest = jax.random.permutation(jax.random.fold_in(key, 101), span - 1)[:N_SEQ - 1].astype(jnp.int32)
    query_vals = jnp.concatenate([jnp.array([span - 1], jnp.int32), query_rest])
    query_order = jax.random.permutation(jax.random.fold_in(key, 104), query_vals).astype(jnp.int32)
    key_rest = (jax.random.permutation(jax.random.fold_in(key, 102), span - 2)[:N_SEQ - 2] + 1).astype(jnp.int32)
    key_vals = jnp.concatenate([jnp.array([0, span - 1], jnp.int32), key_rest])
    key_order = jax.random.permutation(jax.random.fold_in(key, 105), key_vals).astype(jnp.int32)
    return (query_order, key_order)


def draw_query_blocks(key, part):
    return shared_orders(key)[0]


def draw_key_blocks(key, part):
    return shared_orders(key)[1]


def draw_latent_cache(key, part):
    key = jax.random.fold_in(key, 7)
    base = jnp.clip(jax.random.normal(key, (SEQLEN, DK), jnp.float32), -5.0, 5.0)
    return base.astype(jnp.bfloat16)


def draw_queries(key, part):
    key = jax.random.fold_in(key, 8)
    base = jnp.clip(jax.random.normal(key, (SEQLEN, H, DK), jnp.float32), -5.0, 5.0)
    return base.astype(jnp.bfloat16)


def block_scale(own_key, dims, split, least, high):
    loudness, own = 1.0, jax.random.fold_in(own_key, 6)
    for axis_at, shards_of in split:
        steps = jnp.exp(jax.random.uniform(jax.random.fold_in(own, axis_at), (shards_of,), jnp.float32, least / len(split), high / len(split)))
        loudness = loudness * jnp.repeat(steps, dims[axis_at] // shards_of).reshape([-1 if axis == axis_at else 1 for axis in range(len(dims))])
    return loudness


def scatter_about(stream_key, shape, scale, most, shards=(), kind=jnp.bfloat16):
    gain = block_scale(stream_key, shape, shards, -0.22, 0.18) if shards else 1.0
    values = jax.random.normal(stream_key, shape, jnp.float32) * scale * gain
    return jnp.minimum(jnp.maximum(values, -most), most).astype(kind)


def setup_inputs(seed: int = 0) -> dict:
    keys = jax.random.split(jax.random.key(seed), 6)
    return {
        "queries": draw_queries(jax.random.fold_in(keys[5], 71), 0),
        "latent_cache": draw_latent_cache(jax.random.fold_in(keys[5], 71), 0),
        "grad_output": scatter_about(keys[2], (SEQLEN, H, DL), 1.0, 6.0, ((0, 8), (1, 32))),
        "query_blocks": draw_query_blocks(jax.random.fold_in(keys[5], 71), 0),
        "key_blocks": draw_key_blocks(jax.random.fold_in(keys[5], 71), 0),
    }


softmax_scale = 0.07216878364870322


def group_terms(q_tile, g_tile, query_pos, latent_cache, key_pos):
    cache_f = latent_cache.astype(jnp.float32)
    values = cache_f[:, :DL]
    scores = softmax_scale * jnp.einsum('qhd,kd->qhk', q_tile.astype(jnp.float32), cache_f)
    visible = key_pos[None, None, :] <= query_pos[:, None, None]
    masked = jnp.where(visible, scores, -jnp.inf)
    row_max = jnp.max(masked, axis=-1, keepdims=True)
    weights = jnp.exp(masked - row_max)
    probability = weights / jnp.sum(weights, axis=-1, keepdims=True)
    prob_bf16 = probability.astype(jnp.bfloat16).astype(jnp.float32)
    grad_f = g_tile.astype(jnp.float32)
    output = jnp.einsum('qhk,ke->qhe', prob_bf16, values)
    correction = jnp.sum(grad_f * output, axis=-1, keepdims=True)
    grad_probs = jnp.einsum('qhe,ke->qhk', grad_f, values)
    grad_scores = (softmax_scale * probability * (grad_probs - correction)).astype(jnp.bfloat16).astype(jnp.float32)
    grad_tile = jnp.einsum('qhk,kd->qhd', grad_scores, cache_f).astype(jnp.bfloat16)
    grad_keys = jnp.einsum('qhk,qhd->kd', grad_scores, q_tile.astype(jnp.float32))
    grad_values = jnp.einsum('qhk,qhe->ke', prob_bf16, grad_f)
    zeros_rope = jnp.zeros((grad_values.shape[0], DR), jnp.float32)
    return grad_tile, grad_keys + jnp.concatenate([grad_values, zeros_rope], axis=1)


def reference(queries, latent_cache, grad_output, query_blocks, key_blocks):
    offsets = jnp.arange(TILE, dtype=jnp.int32)
    key_pos = (key_blocks[:, None] * TILE + offsets[None, :]).reshape(-1)
    query_pos = query_blocks[:, None] * TILE + offsets[None, :]
    tiles = queries.reshape(N_SEQ, TILE, H, DK)
    grads = grad_output.reshape(N_SEQ, TILE, H, DL)

    def advance(carry, inputs):
        q_tile, g_tile, positions = inputs
        grad_tile, grad_part = group_terms(q_tile, g_tile, positions, latent_cache, key_pos)
        return carry + grad_part, grad_tile

    start = jnp.zeros((SEQLEN, DK), jnp.float32)
    grad_cache, grad_tiles = lax.scan(advance, start, (tiles, grads, query_pos))
    return grad_tiles.reshape(SEQLEN, H, DK), grad_cache
```

```python
import functools

import jax
import jax.numpy as jnp
import numpy as np
from jax import lax
from jax.experimental import pallas as pl
from jax.experimental.pallas import tpu as pltpu
from jax.sharding import Mesh
from jax.sharding import PartitionSpec as P

H_LOC = 4
DL = 512
DR = 64
DK = 576
TILE = 256
HALF = 128
NG = 8
KEYS = NG * TILE
LOG2E = 1.4426950408889634

softmax_scale = 0.07216878364870322

BF = jnp.bfloat16
F32 = jnp.float32


def dot(a, b):
    return lax.dot_general(a, b, (((1,), (0,)), ((), ())), preferred_element_type=F32)


def dot_nt(a, b):
    return lax.dot_general(a, b, (((1,), (1,)), ((), ())), preferred_element_type=F32)


def attn_kernel(
    limit_ref, qt_ref, go_ref, k0_ref, k1_ref,
    dqt_ref, own_ref, other_ref,
    kt_s, k_s, s_s, gp_s, w_s, gl_s, gr_s, delta_s,
):
    head = pl.program_id(0)
    chunks = KEYS // TILE

    @pl.when(head == 0)
    def _():
        for half, ref in enumerate((k0_ref, k1_ref)):
            for group in range(NG):
                at = half * NG * HALF + group * HALF
                block = ref[group]
                kt_s[:, at : at + HALF] = block
                k_s[at : at + HALF, :] = block.T
        t = lax.broadcasted_iota(jnp.int32, (HALF, TILE), 0)
        i = lax.broadcasted_iota(jnp.int32, (HALF, TILE), 1)
        delta_s[...] = (t // 8) * 16 + t % 8 - i

    qt = qt_ref[0]
    go = go_ref[0]
    gl_s[pl.ds(head * 2 * TILE, TILE), :] = go
    q = qt.T
    gl_s[pl.ds(head * 2 * TILE + TILE, TILE), :] = q[:, :DL]
    gr_s[pl.ds(head * TILE, TILE), :] = q[:, DL:]
    got = go.T

    delta = delta_s[...]
    peak = jnp.full((1, TILE), -jnp.inf, F32)
    for c in range(chunks):
        rows = slice(c * TILE, (c + 1) * TILE)
        scores = dot(k_s[rows, :], qt) * (softmax_scale * LOG2E)
        parts = []
        for b in range(2):
            part = scores[b * HALF : (b + 1) * HALF]
            part = jnp.where(delta <= limit_ref[2 * c + b], part, -jnp.inf)
            s_s[c * TILE + b * HALF : c * TILE + (b + 1) * HALF, :] = part
            peak = jnp.maximum(peak, jnp.max(part, axis=0, keepdims=True))
        gp_s[rows, :] = dot(k_s[rows, :DL], got)
    total = jnp.zeros((1, TILE), F32)
    for c in range(chunks):
        rows = slice(c * TILE, (c + 1) * TILE)
        e = jnp.exp2(s_s[rows, :] - peak)
        s_s[rows, :] = e
        total = total + jnp.sum(e, axis=0, keepdims=True)
    inv = 1.0 / total
    corr = jnp.zeros((1, TILE), F32)
    for c in range(chunks):
        rows = slice(c * TILE, (c + 1) * TILE)
        pb = (s_s[rows, :] * inv).astype(BF)
        w_s[rows, pl.ds(head * 2 * TILE, TILE)] = pb
        corr = corr + jnp.sum(pb.astype(F32) * gp_s[rows, :], axis=0, keepdims=True)
    inv_scale = inv * softmax_scale
    dqt = jnp.zeros((DK, TILE), F32)
    for c in range(chunks):
        rows = slice(c * TILE, (c + 1) * TILE)
        ds = (s_s[rows, :] * inv_scale * (gp_s[rows, :] - corr)).astype(BF)
        w_s[rows, pl.ds(head * 2 * TILE + TILE, TILE)] = ds
        dqt = dqt + dot(kt_s[:, rows], ds)
    dqt_ref[0] = dqt.astype(BF)

    @pl.when(head == H_LOC - 1)
    def _():
        for c in range(chunks):
            rows = slice(c * TILE, (c + 1) * TILE)
            w = w_s[rows, :]
            lat = dot(w, gl_s[...])
            wr = jnp.concatenate(
                [w[:, (2 * h + 1) * TILE : (2 * h + 2) * TILE] for h in range(H_LOC)], axis=1
            )
            rope = dot(wr, gr_s[...])
            if c < chunks // 2:
                own_ref[rows, :DL] = lat
                own_ref[rows, DL:] = rope
            else:
                to = slice((c - chunks // 2) * TILE, (c + 1 - chunks // 2) * TILE)
                other_ref[to, :DL] = lat.astype(BF)
                other_ref[to, DL:] = rope.astype(BF)


def attention(limits, qt, go, k_own, k_other):
    whole = lambda *shape: pl.BlockSpec(shape, lambda h: (0,) * len(shape))
    return pl.pallas_call(
        attn_kernel,
        grid=(H_LOC,),
        in_specs=[
            pl.BlockSpec(memory_space=pltpu.SMEM),
            pl.BlockSpec((1, DK, TILE), lambda h: (h, 0, 0)),
            pl.BlockSpec((1, TILE, DL), lambda h: (h, 0, 0)),
            whole(NG, DK, HALF),
            whole(NG, DK, HALF),
        ],
        out_specs=[
            pl.BlockSpec((1, DK, TILE), lambda h: (h, 0, 0)),
            whole(KEYS // 2, DK),
            whole(KEYS // 2, DK),
        ],
        out_shape=[
            jax.ShapeDtypeStruct((H_LOC, DK, TILE), BF),
            jax.ShapeDtypeStruct((KEYS // 2, DK), F32),
            jax.ShapeDtypeStruct((KEYS // 2, DK), BF),
        ],
        scratch_shapes=[
            pltpu.VMEM((DK, KEYS), BF),
            pltpu.VMEM((KEYS, DK), BF),
            pltpu.VMEM((KEYS, TILE), F32),
            pltpu.VMEM((KEYS, TILE), F32),
            pltpu.VMEM((KEYS, H_LOC * 2 * TILE), BF),
            pltpu.VMEM((H_LOC * 2 * TILE, DL), BF),
            pltpu.VMEM((H_LOC * TILE, DR), BF),
            pltpu.VMEM((HALF, TILE), jnp.int32),
        ],
        compiler_params=pltpu.CompilerParams(vmem_limit_bytes=48 * 1024 * 1024),
    )(limits, qt, go, k_own, k_other)


def swap_cores(x):
    return lax.ppermute(x, "c", [(0, 1), (1, 0)])


def shards(queries, latent_cache, grad_output, query_blocks, key_blocks):
    core = lax.axis_index("c")
    group = lax.axis_index("y") * 2 + lax.axis_index("zl")
    row = lax.broadcasted_iota(jnp.int32, (TILE, HALF), 0)
    t = lax.broadcasted_iota(jnp.int32, (TILE, HALF), 1)
    pick = (row == (t // 8) * 16 + core * 8 + t % 8).astype(BF)
    mine = lax.dot_general(
        latent_cache, pick, (((0,), (0,)), ((), ())), preferred_element_type=F32
    ).astype(BF)
    sent = jnp.broadcast_to(mine[None], (NG, DK, HALF))
    k_own = lax.all_to_all(sent, ("y", "zl"), 0, 0, tiled=True)
    k_other = swap_cores(k_own)

    qt = queries.transpose(1, 2, 0)
    go = grad_output.transpose(1, 0, 2)
    lag = (query_blocks[group] - key_blocks) * TILE
    limits = jnp.concatenate([lag - core * 8, lag - (1 - core) * 8])
    dqt, own, other = attention(limits, qt, go, k_own, k_other)

    chip = (own + swap_cores(other).astype(F32)).astype(BF)
    got = lax.all_to_all(chip.reshape(32, 32, DK), ("y", "zl", "x"), 0, 0, tiled=True)
    part = jnp.sum(got.astype(F32), axis=0).astype(BF)
    got = lax.all_to_all(part.reshape(4, 8, DK), "zh", 0, 0, tiled=True)
    return dqt.transpose(2, 0, 1), jnp.sum(got.astype(F32), axis=0)


def solution(mesh):
    fine = Mesh(mesh.devices.reshape(4, 2, 4, 4, 2), ("y", "zl", "x", "zh", "c"))
    seq, head = ("y", "zl"), ("x", "zh", "c")
    placed = (P(seq, head, None), P(seq, None), P(seq, head, None), P(), P())
    return jax.shard_map(
        shards,
        mesh=fine,
        in_specs=placed,
        out_specs=(P(seq, head, None), P(seq + head, None)),
        check_vma=False,
    )
```

```python
import functools

import jax
import jax.numpy as jnp
import numpy as np
from jax import lax
from jax.experimental import pallas as pl
from jax.experimental.pallas import tpu as pltpu
from jax.sharding import Mesh
from jax.sharding import PartitionSpec as P

H_LOC = 4
DL = 512
DR = 64
DK = 576
TILE = 256
HALF = 128
NG = 8
KEYS = NG * TILE
LOG2E = 1.4426950408889634
LOW = -jnp.inf
FLOOR = -1e30
SLOTS = ((0, 0), (2, 1), (2, 0), (1, 1), (3, 1), (1, 0), (3, 0), (0, 1))
LANES = 128
OWNED = 32
PACKED = OWNED * DK // LANES
OWN_TYPE = jnp.float32
VMEM_LIMIT = 44 * 1024 * 1024

softmax_scale = 0.07216878364870322

BF = jnp.bfloat16
F32 = jnp.float32


def dot(a, b):
    return lax.dot_general(a, b, (((1,), (0,)), ((), ())), preferred_element_type=F32)


def dot_nt(a, b):
    return lax.dot_general(a, b, (((1,), (1,)), ((), ())), preferred_element_type=F32)


def attn_kernel(
    place_ref, query_blocks_ref, key_blocks_ref, qt_ref, go_ref, *refs
):
    k_refs = refs[: 2 * NG]
    dqt_ref, own_ref, other_ref, kt_s, k_s, e_s, gp_s, w_s, gl_s, gr_s, got_s = refs[2 * NG :]
    chunks = KEYS // TILE
    core, y, zl = (place_ref[n] for n in range(3))
    groups = [((y - dy) & 3) * 2 + (zl ^ dz) for dy, dz in SLOTS]
    lags = [(query_blocks_ref[groups[0]] - key_blocks_ref[g]) * TILE for g in groups]
    limits = [lag - (core ^ half) * 8 for half in range(2) for lag in lags]
    for n, ref in enumerate(k_refs):
        block = ref[...]
        kt_s[:, n * HALF : (n + 1) * HALF] = block
        k_s[n * HALF : (n + 1) * HALF, :] = block.T
    t = lax.broadcasted_iota(jnp.int32, (HALF, TILE), 0)
    i = lax.broadcasted_iota(jnp.int32, (HALF, TILE), 1)
    delta = (t >> 3) * 16 + (t & 7) - i

    peaks = [[None] * chunks for _ in range(H_LOC)]
    sums = [[None] * chunks for _ in range(H_LOC)]
    factors = [None] * H_LOC
    corrs = [None] * H_LOC

    def span(c):
        return slice(c * TILE, (c + 1) * TILE)

    def load(h):
        go = go_ref[h]
        gl_s[h * 2 * TILE : h * 2 * TILE + TILE, :] = go
        got_s[h] = go.T
        q = qt_ref[h].T
        gl_s[h * 2 * TILE + TILE : (h + 1) * 2 * TILE, :] = q[:, :DL]
        gr_s[h * TILE : (h + 1) * TILE, :] = q[:, DL:]

    def weigh(h, c):
        scores = dot(k_s[span(c), :], qt_ref[h]) * (softmax_scale * LOG2E)
        parts = [
            jnp.where(delta <= limits[2 * c + b], scores[b * HALF : (b + 1) * HALF], LOW)
            for b in range(2)
        ]
        peak = jnp.maximum(*[jnp.max(p, axis=0, keepdims=True) for p in parts])
        total = jnp.zeros((1, TILE), F32)
        for b in range(2):
            e = jnp.exp2(parts[b] - jnp.maximum(peak, FLOOR))
            e_s[h, c * TILE + b * HALF : c * TILE + (b + 1) * HALF, :] = e
            total = total + jnp.sum(e, axis=0, keepdims=True)
        peaks[h][c] = peak
        sums[h][c] = total
        gp_s[h, span(c), :] = dot(k_s[span(c), :DL], got_s[h])

    def settle(h):
        peak = functools.reduce(jnp.maximum, peaks[h])
        shares = [jnp.exp2(p - peak) for p in peaks[h]]
        inv = 1.0 / sum(f * s for f, s in zip(shares, sums[h]))
        factors[h] = [f * inv for f in shares]
        corrs[h] = jnp.zeros((1, TILE), F32)

    def correct(h, c):
        pb = (e_s[h, span(c), :] * factors[h][c]).astype(BF)
        w_s[span(c), h * 2 * TILE : h * 2 * TILE + TILE] = pb
        corrs[h] = corrs[h] + jnp.sum(pb.astype(F32) * gp_s[h, span(c), :], axis=0, keepdims=True)

    def differ(h, c):
        p = e_s[h, span(c), :] * (factors[h][c] * softmax_scale)
        ds = (p * (gp_s[h, span(c), :] - corrs[h])).astype(BF)
        w_s[span(c), h * 2 * TILE + TILE : (h + 1) * 2 * TILE] = ds

    def to_queries(h):
        for r in range(2):
            rows = slice(r * DK // 2, (r + 1) * DK // 2)
            out = dot(kt_s[rows, :], w_s[:, h * 2 * TILE + TILE : (h + 1) * 2 * TILE])
            dqt_ref[h, rows, :] = out.astype(BF)

    def to_keys(c):
        w = w_s[span(c), :]
        lat = dot(w, gl_s[...])
        wr = jnp.concatenate(
            [w[:, (2 * h + 1) * TILE : (2 * h + 2) * TILE] for h in range(H_LOC)], axis=1
        )
        rope = dot(wr, gr_s[...])
        ref = own_ref if c < chunks // 2 else other_ref
        for b in range(2):
            group = groups[(2 * c + b) % NG]
            for x in range(4):
                at = b * HALF + x * OWNED
                to = group * 4 + x
                for n in range(DL // LANES):
                    ref[to, n * OWNED : (n + 1) * OWNED, :] = lat[
                        at : at + OWNED, n * LANES : (n + 1) * LANES
                    ].astype(ref.dtype)
                both = jnp.concatenate(
                    [rope[at : at + OWNED // 2], rope[at + OWNED // 2 : at + OWNED]], axis=1
                )
                ref[to, DL // LANES * OWNED :, :] = both.astype(ref.dtype)

    for step in range(H_LOC + 2):
        if step < H_LOC:
            load(step)
        if 1 <= step <= H_LOC:
            settle(step - 1)
        for c in range(chunks):
            if step < H_LOC:
                weigh(step, c)
            if 1 <= step <= H_LOC:
                correct(step - 1, c)
            if step >= 2:
                differ(step - 2, c)
        if step >= 2:
            to_queries(step - 2)
    for c in range(chunks):
        to_keys(c)


def attention(place, query_blocks, key_blocks, qt, go, k_blocks):
    vmem = pl.BlockSpec(memory_space=pltpu.VMEM)
    smem = pl.BlockSpec(memory_space=pltpu.SMEM)
    return pl.pallas_call(
        attn_kernel,
        in_specs=[smem] * 3 + [vmem] * (2 + len(k_blocks)),
        out_specs=[vmem] * 3,
        out_shape=[
            jax.ShapeDtypeStruct((H_LOC, DK, TILE), BF),
            jax.ShapeDtypeStruct((NG * 4, PACKED, LANES), OWN_TYPE),
            jax.ShapeDtypeStruct((NG * 4, PACKED, LANES), BF),
        ],
        scratch_shapes=[
            pltpu.VMEM((DK, KEYS), BF),
            pltpu.VMEM((KEYS, DK), BF),
            pltpu.VMEM((H_LOC, KEYS, TILE), F32),
            pltpu.VMEM((H_LOC, KEYS, TILE), F32),
            pltpu.VMEM((KEYS, H_LOC * 2 * TILE), BF),
            pltpu.VMEM((H_LOC * 2 * TILE, DL), BF),
            pltpu.VMEM((H_LOC * TILE, DR), BF),
            pltpu.VMEM((H_LOC, DL, TILE), BF),
        ],
        compiler_params=pltpu.CompilerParams(vmem_limit_bytes=VMEM_LIMIT),
    )(place, query_blocks, key_blocks, qt, go, *k_blocks)


def swap_cores(x):
    return lax.ppermute(x, "c", [(0, 1), (1, 0)])


def from_group(x, dy, dz):
    pairs = [(y * 2 + z, (y + dy) % 4 * 2 + (z ^ dz)) for y in range(4) for z in range(2)]
    return lax.ppermute(x, ("y", "zl"), pairs)


def unpack(x):
    lat = x[: DL // LANES * OWNED].reshape(DL // LANES, 4, 8, LANES)
    lat = lat.transpose(1, 2, 0, 3).reshape(4, 8, DL)
    rope = x[DL // LANES * OWNED :].reshape(2, 8, 2, DR).transpose(2, 0, 1, 3).reshape(4, 8, DR)
    return jnp.concatenate([lat, rope], axis=2)


def shards(queries, latent_cache, grad_output, query_blocks, key_blocks):
    core, y, zl = (lax.axis_index(a) for a in ("c", "y", "zl"))
    row = lax.broadcasted_iota(jnp.int32, (TILE, TILE), 0)
    t = lax.broadcasted_iota(jnp.int32, (TILE, TILE), 1)
    half, t = t >> 7, t & 127
    pick = (row == (t >> 3) * 16 + (core ^ half) * 8 + (t & 7)).astype(BF)
    here = lax.dot_general(
        latent_cache, pick, (((0,), (0,)), ((), ())), preferred_element_type=F32
    ).astype(BF)
    mine = here[:, :HALF]
    k_own = [from_group(mine, dy, dz) for dy, dz in SLOTS[1:]]
    k_other = [swap_cores(k) for k in k_own]
    qt = queries.transpose(1, 2, 0)
    go = grad_output.transpose(1, 0, 2)
    blocks = [mine] + k_own + [here[:, HALF:]] + k_other
    dqt, own, other = attention(
        jnp.stack([core, y, zl]), query_blocks, key_blocks, qt, go, blocks
    )

    chip = (own + swap_cores(other).astype(F32)).astype(BF)
    got = lax.all_to_all(chip, ("y", "zl", "x"), 0, 0, tiled=True)
    part = unpack(jnp.sum(got.astype(F32), axis=0)).astype(BF)
    got = lax.all_to_all(part, "zh", 0, 0, tiled=True)
    return dqt.transpose(2, 0, 1), jnp.sum(got.astype(F32), axis=0)


def solution(mesh):
    fine = Mesh(mesh.devices.reshape(4, 2, 4, 4, 2), ("y", "zl", "x", "zh", "c"))
    seq, head = ("y", "zl"), ("x", "zh", "c")
    placed = (P(seq, head, None), P(seq, None), P(seq, head, None), P(), P())
    return jax.shard_map(
        shards,
        mesh=fine,
        in_specs=placed,
        out_specs=(P(seq, head, None), P(seq + head, None)),
        check_vma=False,
    )
```

```python
import functools

import jax
import jax.numpy as jnp
import numpy as np
from jax import lax
from jax.experimental import pallas as pl
from jax.experimental.pallas import tpu as pltpu
from jax.sharding import Mesh
from jax.sharding import PartitionSpec as P

H_LOC = 4
DL = 512
DR = 64
DK = 576
TILE = 256
HALF = 128
NG = 8
KEYS = NG * TILE
LOG2E = 1.4426950408889634
LOW = -jnp.inf
FLOOR = -1e30
K_ROWS = ((0, 1), (0, 1), (1, 0), (0, 1), (1, 0), (0, None), (0, None), (0, None)) + ((None, 0),) * 3
LANES = 128
OWNED = 32
PACKED = OWNED * DK // LANES
OWN_TYPE = jnp.float32
VMEM_LIMIT = 44 * 1024 * 1024

softmax_scale = 0.07216878364870322

BF = jnp.bfloat16
F32 = jnp.float32


def dot(a, b):
    return lax.dot_general(a, b, (((1,), (0,)), ((), ())), preferred_element_type=F32)


def dot_nt(a, b):
    return lax.dot_general(a, b, (((1,), (1,)), ((), ())), preferred_element_type=F32)


def attn_kernel(
    place_ref, query_blocks_ref, key_blocks_ref, qt_ref, go_ref, *refs
):
    k_refs = refs[: len(K_ROWS)]
    dqt_ref, own_ref, other_ref, kt_s, k_s, e_s, gp_s, w_s, gl_s, gr_s, got_s = refs[len(K_ROWS) :]
    chunks = KEYS // TILE
    core, y, zl, x = (place_ref[n] for n in range(4))
    behind = (0, 1 + 2 * core, 3 - 2 * core, 1 + 2 * core, 3 - 2 * core, 0, 2, 2)
    across = (0, 0, 0, 1, 1, 1, 0, 1)
    ahead = [(0 - dy) & 3 for dy in behind]
    floors = [zl ^ dz for dz in across]
    groups = [((y + up) & 3) * 2 + z for up, z in zip(ahead, floors)]
    lags = [(query_blocks_ref[groups[0]] - key_blocks_ref[g]) * TILE for g in groups]
    limits = [lag - (core ^ half) * 8 for half in range(2) for lag in lags]
    n = 0
    for half in range(2):
        for ref, rows in zip(k_refs, K_ROWS):
            if rows[half] is None:
                continue
            block = ref[rows[half] * DK : (rows[half] + 1) * DK, :]
            kt_s[:, n * HALF : (n + 1) * HALF] = block
            k_s[n * HALF : (n + 1) * HALF, :] = block.T
            n += 1
    t = lax.broadcasted_iota(jnp.int32, (HALF, TILE), 0)
    i = lax.broadcasted_iota(jnp.int32, (HALF, TILE), 1)
    delta = (t >> 3) * 16 + (t & 7) - i

    peaks = [[None] * chunks for _ in range(H_LOC)]
    sums = [[None] * chunks for _ in range(H_LOC)]
    factors = [None] * H_LOC
    corrs = [None] * H_LOC

    def span(c):
        return slice(c * TILE, (c + 1) * TILE)

    def load(h):
        go = go_ref[h]
        gl_s[h * 2 * TILE : h * 2 * TILE + TILE, :] = go
        got_s[h] = go.T
        q = qt_ref[h].T
        gl_s[h * 2 * TILE + TILE : (h + 1) * 2 * TILE, :] = q[:, :DL]
        gr_s[h * TILE : (h + 1) * TILE, :] = q[:, DL:]

    def weigh(h, c):
        scores = dot(k_s[span(c), :], qt_ref[h]) * (softmax_scale * LOG2E)
        parts = [
            jnp.where(delta <= limits[2 * c + b], scores[b * HALF : (b + 1) * HALF], LOW)
            for b in range(2)
        ]
        peak = jnp.maximum(*[jnp.max(p, axis=0, keepdims=True) for p in parts])
        total = jnp.zeros((1, TILE), F32)
        for b in range(2):
            e = jnp.exp2(parts[b] - jnp.maximum(peak, FLOOR))
            e_s[h, c * TILE + b * HALF : c * TILE + (b + 1) * HALF, :] = e
            total = total + jnp.sum(e, axis=0, keepdims=True)
        peaks[h][c] = peak
        sums[h][c] = total
        gp_s[h, span(c), :] = dot(k_s[span(c), :DL], got_s[h])

    def settle(h):
        peak = functools.reduce(jnp.maximum, peaks[h])
        shares = [jnp.exp2(p - peak) for p in peaks[h]]
        inv = 1.0 / sum(f * s for f, s in zip(shares, sums[h]))
        factors[h] = [f * inv for f in shares]
        corrs[h] = jnp.zeros((1, TILE), F32)

    def correct(h, c):
        pb = (e_s[h, span(c), :] * factors[h][c]).astype(BF)
        w_s[span(c), h * 2 * TILE : h * 2 * TILE + TILE] = pb
        corrs[h] = corrs[h] + jnp.sum(pb.astype(F32) * gp_s[h, span(c), :], axis=0, keepdims=True)

    def differ(h, c):
        p = e_s[h, span(c), :] * (factors[h][c] * softmax_scale)
        ds = (p * (gp_s[h, span(c), :] - corrs[h])).astype(BF)
        w_s[span(c), h * 2 * TILE + TILE : (h + 1) * 2 * TILE] = ds

    def to_queries(h):
        for r in range(2):
            rows = slice(r * DK // 2, (r + 1) * DK // 2)
            out = dot(kt_s[rows, :], w_s[:, h * 2 * TILE + TILE : (h + 1) * 2 * TILE])
            dqt_ref[h, rows, :] = out.astype(BF)

    def to_keys(c):
        w = w_s[span(c), :]
        lat = dot(w, gl_s[...])
        wr = jnp.concatenate(
            [w[:, (2 * h + 1) * TILE : (2 * h + 2) * TILE] for h in range(H_LOC)], axis=1
        )
        rope = dot(wr, gr_s[...])
        ref = own_ref if c < chunks // 2 else other_ref
        for b in range(2):
            up, floor = ahead[(2 * c + b) % NG], floors[(2 * c + b) % NG]
            for to in range(4):
                at = b * HALF + to * OWNED
                right = (to - x) & 3
                i = jnp.where(floor == 0, right, up)
                j = jnp.where(floor == 0, up, right)
                for n in range(DL // LANES):
                    ref[floor, i, j, n * OWNED : (n + 1) * OWNED, :] = lat[
                        at : at + OWNED, n * LANES : (n + 1) * LANES
                    ].astype(ref.dtype)
                both = jnp.concatenate(
                    [rope[at : at + OWNED // 2], rope[at + OWNED // 2 : at + OWNED]], axis=1
                )
                ref[floor, i, j, DL // LANES * OWNED :, :] = both.astype(ref.dtype)

    for step in range(H_LOC + 2):
        if step < H_LOC:
            load(step)
        if 1 <= step <= H_LOC:
            settle(step - 1)
        for c in range(chunks):
            if step < H_LOC:
                weigh(step, c)
            if 1 <= step <= H_LOC:
                correct(step - 1, c)
            if step >= 2:
                differ(step - 2, c)
        if step >= 2:
            to_queries(step - 2)
    for c in range(chunks):
        to_keys(c)


def attention(place, query_blocks, key_blocks, qt, go, k_blocks):
    vmem = pl.BlockSpec(memory_space=pltpu.VMEM)
    smem = pl.BlockSpec(memory_space=pltpu.SMEM)
    return pl.pallas_call(
        attn_kernel,
        in_specs=[smem] * 3 + [vmem] * (2 + len(k_blocks)),
        out_specs=[vmem] * 3,
        out_shape=[
            jax.ShapeDtypeStruct((H_LOC, DK, TILE), BF),
            jax.ShapeDtypeStruct((2, 4, 4, PACKED, LANES), OWN_TYPE),
            jax.ShapeDtypeStruct((2, 4, 4, PACKED, LANES), BF),
        ],
        scratch_shapes=[
            pltpu.VMEM((DK, KEYS), BF),
            pltpu.VMEM((KEYS, DK), BF),
            pltpu.VMEM((H_LOC, KEYS, TILE), F32),
            pltpu.VMEM((H_LOC, KEYS, TILE), F32),
            pltpu.VMEM((KEYS, H_LOC * 2 * TILE), BF),
            pltpu.VMEM((H_LOC * 2 * TILE, DL), BF),
            pltpu.VMEM((H_LOC * TILE, DR), BF),
            pltpu.VMEM((H_LOC, DL, TILE), BF),
        ],
        compiler_params=pltpu.CompilerParams(vmem_limit_bytes=VMEM_LIMIT),
    )(place, query_blocks, key_blocks, qt, go, *k_blocks)


def swap_cores(x):
    return lax.ppermute(x, "c", [(0, 1), (1, 0)])


def onward(x, dz):
    pairs = [
        ((y * 2 + z) * 2 + c, ((y + 1 - 2 * c) % 4 * 2 + (z ^ dz)) * 2 + c)
        for y in range(4)
        for z in range(2)
        for c in range(2)
    ]
    return lax.ppermute(x, ("y", "zl", "c"), pairs)


def shift(x, axis, step):
    return lax.ppermute(x, axis, [(n, (n + step) % 4) for n in range(4)])


def unpack(x):
    lat = x[: DL // LANES * OWNED].reshape(DL // LANES, 4, 8, LANES)
    lat = lat.transpose(1, 2, 0, 3).reshape(4, 8, DL)
    rope = x[DL // LANES * OWNED :].reshape(2, 8, 2, DR).transpose(2, 0, 1, 3).reshape(4, 8, DR)
    return jnp.concatenate([lat, rope], axis=2)


def shards(queries, latent_cache, grad_output, query_blocks, key_blocks):
    core, y, zl, x = (lax.axis_index(a) for a in ("c", "y", "zl", "x"))
    row = lax.broadcasted_iota(jnp.int32, (TILE, TILE), 0)
    t = lax.broadcasted_iota(jnp.int32, (TILE, TILE), 1)
    half, t = t >> 7, t & 127
    pick = (row == (t >> 3) * 16 + (core ^ half) * 8 + (t & 7)).astype(BF)
    here = lax.dot_general(
        latent_cache, pick, (((0,), (0,)), ((), ())), preferred_element_type=F32
    ).astype(BF)
    here = jnp.concatenate([here[:, :HALF], here[:, HALF:]], axis=0)

    near = onward(here, 0)
    slant = onward(here, 1)
    beside = lax.ppermute(here[:DK], "zl", [(0, 1), (1, 0)])
    far = onward(near[:DK], 0)
    far_slant = onward(slant[:DK], 0)
    singles = [beside, far, far_slant]
    blocks = [here, near, swap_cores(near), slant, swap_cores(slant)]
    blocks += singles + [swap_cores(k) for k in singles]

    qt = queries.transpose(1, 2, 0)
    go = grad_output.transpose(1, 0, 2)
    place = jnp.stack([core, y, zl, x])
    dqt, own, other = attention(place, query_blocks, key_blocks, qt, go, blocks)

    other = swap_cores(other)
    sums = [[own[h, d] + other[h, d].astype(F32) for d in range(4)] for h in range(2)]
    for axes in (("x", "y"), ("y", "x")):
        got = [
            [shift(sums[h][d].astype(BF), axes[h], d).astype(F32) for h in range(2)]
            for d in (2, 1, 3)
        ]
        sums = [sums[h][0] + sum(g[h] for g in got) for h in range(2)]
    part = jnp.concatenate([unpack(s).astype(BF) for s in sums], axis=0)
    got = lax.all_to_all(part, ("zl", "zh"), 0, 0, tiled=True)
    return dqt.transpose(2, 0, 1), jnp.sum(got.astype(F32), axis=0)


def solution(mesh):
    fine = Mesh(mesh.devices.reshape(4, 2, 4, 4, 2), ("y", "zl", "x", "zh", "c"))
    seq, head = ("y", "zl"), ("x", "zh", "c")
    placed = (P(seq, head, None), P(seq, None), P(seq, head, None), P(), P())
    return jax.shard_map(
        shards,
        mesh=fine,
        in_specs=placed,
        out_specs=(P(seq, head, None), P(seq + head, None)),
        check_vma=False,
    )
```

```python
import functools

import jax
import jax.numpy as jnp
import numpy as np
from jax import lax
from jax.experimental import pallas as pl
from jax.experimental.pallas import tpu as pltpu
from jax.sharding import Mesh
from jax.sharding import PartitionSpec as P

H_LOC = 4
DL = 512
DR = 64
DK = 576
TILE = 256
HALF = 128
NG = 8
KEYS = NG * TILE
LOG2E = 1.4426950408889634
FLOOR = -1e30
LANES = 128
OWNED = 32
PACKED = OWNED * DK // LANES
MAIN_VMEM = 28 * 1024 * 1024
FIRST = 5
SWAPPED = (2, 4)

softmax_scale = 0.07216878364870322

BF = jnp.bfloat16
F32 = jnp.float32


def dot(a, b):
    return lax.dot_general(a, b, (((1,), (0,)), ((), ())), preferred_element_type=F32)


def dot_nt(a, b):
    return lax.dot_general(a, b, (((1,), (1,)), ((), ())), preferred_element_type=F32)


def positions(place_ref, query_blocks_ref, key_blocks_ref):
    core, y, zl = (place_ref[n] for n in range(3))
    turn = 2 * core
    ahead = [(0 - dy) & 3 for dy in (0, 1 + turn, 3 - turn, 1 + turn, 3 - turn, 0, 2, 2)]
    floors = [zl ^ dz for dz in (0, 0, 0, 1, 1, 1, 0, 1)]
    mine = query_blocks_ref[y * 2 + zl]
    limits = []
    for up, floor in zip(ahead, floors):
        lag = (mine - key_blocks_ref[((y + up) & 3) * 2 + floor]) * TILE
        limits.append((lag - core * 8, lag - (core ^ 1) * 8))
    return ahead, floors, limits


def halves(refs):
    out = []
    for slot in range(FIRST):
        flip = slot in SWAPPED
        blocks = [refs[slot][n * DK : (n + 1) * DK, :] for n in range(2)]
        out.append(blocks[::-1] if flip else blocks)
    rest = refs[FIRST:]
    for slot in range(len(rest) // 2):
        out.append([rest[slot][...], rest[slot + len(rest) // 2][...]])
    return out


def offsets():
    t = lax.broadcasted_iota(jnp.int32, (HALF, TILE), 0)
    i = lax.broadcasted_iota(jnp.int32, (HALF, TILE), 1)
    return (t >> 3) * 16 + (t & 7) - i


def span(c):
    return slice(c * TILE, (c + 1) * TILE)


def weigh(keys, qt, got, delta, limits):
    scores = dot(keys, qt) * (softmax_scale * LOG2E)
    parts = [
        jnp.where(delta <= limits[b], scores[b * HALF : (b + 1) * HALF], -jnp.inf)
        for b in range(2)
    ]
    peak = jnp.maximum(*[jnp.max(p, axis=0, keepdims=True) for p in parts])
    floor = jnp.maximum(peak, FLOOR)
    e = [jnp.exp2(p - floor) for p in parts]
    total = sum(jnp.sum(p, axis=0, keepdims=True) for p in e)
    return e, dot(keys[:, :DL], got), peak, total


def first_kernel(place_ref, query_blocks_ref, key_blocks_ref, qt_ref, go_ref, *refs):
    e_ref, gp_ref, stat_ref, gl_ref, gr_ref, got_ref, k_s = refs[FIRST:]
    limits = positions(place_ref, query_blocks_ref, key_blocks_ref)[2]
    for slot, pair in enumerate(halves(refs[:FIRST])):
        for b in range(2):
            at = slot * TILE + b * HALF
            k_s[at : at + HALF, :] = pair[b].T
    delta = offsets()
    for h in range(H_LOC):
        go = go_ref[h]
        gl_ref[h * 2 * TILE : h * 2 * TILE + TILE, :] = go
        got_ref[h] = go.T
        q = qt_ref[h].T
        gl_ref[h * 2 * TILE + TILE : (h + 1) * 2 * TILE, :] = q[:, :DL]
        gr_ref[h * TILE : (h + 1) * TILE, :] = q[:, DL:]
        for c in range(FIRST):
            e, gp, peak, total = weigh(k_s[span(c), :], qt_ref[h], got_ref[h], delta, limits[c])
            for b in range(2):
                at = c * TILE + b * HALF
                e_ref[h, at : at + HALF, :] = e[b]
            gp_ref[h, span(c), :] = gp
            stat_ref[0, h, c : c + 1, :] = peak
            stat_ref[1, h, c : c + 1, :] = total


def main_kernel(place_ref, query_blocks_ref, key_blocks_ref, qt_ref, *refs):
    k_refs, refs = refs[: 2 * NG - FIRST], refs[2 * NG - FIRST :]
    e1_ref, gp1_ref, stat_ref, gl_ref, gr_ref, got_ref = refs[:6]
    dqt_ref, own_ref, other_ref, kt_s, k_s, e_s, gp_s, w_s = refs[6:]
    ahead, floors, limits = positions(place_ref, query_blocks_ref, key_blocks_ref)
    core, x = place_ref[0], place_ref[3]
    for slot, pair in enumerate(halves(k_refs)):
        for b in range(2):
            at = slot * TILE + b * HALF
            kt_s[:, at : at + HALF] = pair[b]
            if slot >= FIRST:
                at -= FIRST * TILE
                k_s[at : at + HALF, :] = pair[b].T
    delta = offsets()
    peaks = [[stat_ref[0, h, c : c + 1, :] for c in range(FIRST)] for h in range(H_LOC)]
    sums = [[stat_ref[1, h, c : c + 1, :] for c in range(FIRST)] for h in range(H_LOC)]
    factors = [None] * H_LOC
    corrs = [None] * H_LOC

    def load(h, c):
        if c < FIRST:
            return e1_ref[h, span(c), :], gp1_ref[h, span(c), :]
        return e_s[h, span(c - FIRST), :], gp_s[h, span(c - FIRST), :]

    def settle(h):
        peak = functools.reduce(jnp.maximum, peaks[h])
        shares = [jnp.exp2(p - peak) for p in peaks[h]]
        inv = 1.0 / sum(f * s for f, s in zip(shares, sums[h]))
        factors[h] = [f * inv for f in shares]
        corrs[h] = jnp.zeros((1, TILE), F32)

    def correct(h, c):
        e, gp = load(h, c)
        pb = (e * factors[h][c]).astype(BF)
        w_s[span(c), h * 2 * TILE : h * 2 * TILE + TILE] = pb
        corrs[h] = corrs[h] + jnp.sum(pb.astype(F32) * gp, axis=0, keepdims=True)

    def differ(h, c):
        e, gp = load(h, c)
        ds = (e * (factors[h][c] * softmax_scale) * (gp - corrs[h])).astype(BF)
        w_s[span(c), h * 2 * TILE + TILE : (h + 1) * 2 * TILE] = ds

    def to_queries(h):
        for r in range(2):
            rows = slice(r * DK // 2, (r + 1) * DK // 2)
            out = dot(kt_s[rows, :], w_s[:, h * 2 * TILE + TILE : (h + 1) * 2 * TILE])
            dqt_ref[h, rows, :] = out.astype(BF)

    def to_keys(c):
        w = w_s[span(c), :]
        lat = dot(w, gl_ref[...])
        wr = jnp.concatenate(
            [w[:, (2 * h + 1) * TILE : (2 * h + 2) * TILE] for h in range(H_LOC)], axis=1
        )
        rope = dot(wr, gr_ref[...])
        for b, ref in enumerate((own_ref, other_ref)):
            down = core ^ b
            up = jnp.where(down == 0, ahead[c], 0 - ahead[c]) & 3
            for to in range(4):
                at = b * HALF + to * OWNED
                right = jnp.where(down == 0, to - x, x - to) & 3
                for n in range(DL // LANES):
                    ref[right, up, floors[c], n * OWNED : (n + 1) * OWNED, :] = lat[
                        at : at + OWNED, n * LANES : (n + 1) * LANES
                    ].astype(ref.dtype)
                both = jnp.concatenate(
                    [rope[at : at + OWNED // 2], rope[at + OWNED // 2 : at + OWNED]], axis=1
                )
                ref[right, up, floors[c], DL // LANES * OWNED :, :] = both.astype(ref.dtype)

    for step in range(H_LOC + 2):
        if 1 <= step <= H_LOC:
            settle(step - 1)
        for c in range(NG):
            if step < H_LOC and c >= FIRST:
                e, gp, peak, total = weigh(
                    k_s[span(c - FIRST), :], qt_ref[step], got_ref[step], delta, limits[c]
                )
                for b in range(2):
                    at = (c - FIRST) * TILE + b * HALF
                    e_s[step, at : at + HALF, :] = e[b]
                gp_s[step, span(c - FIRST), :] = gp
                peaks[step].append(peak)
                sums[step].append(total)
            if 1 <= step <= H_LOC:
                correct(step - 1, c)
            if step >= 2:
                differ(step - 2, c)
        if step >= 2:
            to_queries(step - 2)
    for c in range(NG):
        to_keys(c)


VMEM = pl.BlockSpec(memory_space=pltpu.VMEM)
SMEM = pl.BlockSpec(memory_space=pltpu.SMEM)


def first_part(place, query_blocks, key_blocks, qt, go, k_blocks):
    shapes = [
        ((H_LOC, FIRST * TILE, TILE), F32),
        ((H_LOC, FIRST * TILE, TILE), F32),
        ((2, H_LOC, 8, TILE), F32),
        ((H_LOC * 2 * TILE, DL), BF),
        ((H_LOC * TILE, DR), BF),
        ((H_LOC, DL, TILE), BF),
    ]
    return pl.pallas_call(
        first_kernel,
        in_specs=[SMEM] * 3 + [VMEM] * (2 + FIRST),
        out_specs=[VMEM] * len(shapes),
        out_shape=[jax.ShapeDtypeStruct(*s) for s in shapes],
        scratch_shapes=[pltpu.VMEM((FIRST * TILE, DK), BF)],
        cost_estimate=pl.CostEstimate(
            flops=2 * 1024 * FIRST * TILE * (DK + DL), bytes_accessed=20_000_000, transcendentals=0
        ),
        compiler_params=pltpu.CompilerParams(vmem_limit_bytes=24 * 1024 * 1024),
    )(place, query_blocks, key_blocks, qt, go, *k_blocks)


def main_part(place, query_blocks, key_blocks, qt, k_blocks, early):
    rest = (NG - FIRST) * TILE
    return pl.pallas_call(
        main_kernel,
        in_specs=[SMEM] * 3 + [VMEM] * (1 + len(k_blocks) + len(early)),
        out_specs=[VMEM] * 3,
        out_shape=[
            jax.ShapeDtypeStruct((H_LOC, DK, TILE), BF),
            jax.ShapeDtypeStruct((4, 4, 2, PACKED, LANES), F32),
            jax.ShapeDtypeStruct((4, 4, 2, PACKED, LANES), BF),
        ],
        scratch_shapes=[
            pltpu.VMEM((DK, KEYS), BF),
            pltpu.VMEM((rest, DK), BF),
            pltpu.VMEM((H_LOC, rest, TILE), F32),
            pltpu.VMEM((H_LOC, rest, TILE), F32),
            pltpu.VMEM((KEYS, H_LOC * 2 * TILE), BF),
        ],
        compiler_params=pltpu.CompilerParams(vmem_limit_bytes=MAIN_VMEM),
    )(place, query_blocks, key_blocks, qt, *k_blocks, *early)


def swap_cores(x):
    return lax.ppermute(x, "c", [(0, 1), (1, 0)])


def onward(x, dz):
    pairs = [
        ((y * 2 + z) * 2 + c, ((y + 1 - 2 * c) % 4 * 2 + (z ^ dz)) * 2 + c)
        for y in range(4)
        for z in range(2)
        for c in range(2)
    ]
    return lax.ppermute(x, ("y", "zl", "c"), pairs)


def mirrored(x, axis, step):
    pairs = [
        (n * 2 + c, (n + (step if c == 0 else -step)) % 4 * 2 + c)
        for n in range(4)
        for c in range(2)
    ]
    return lax.ppermute(x, (axis, "c"), pairs)


def opposite(x, dz):
    pairs = [(y * 2 + z, (y + 2) % 4 * 2 + (z ^ dz)) for y in range(4) for z in range(2)]
    return lax.ppermute(x, ("y", "zl"), pairs)


def unpack(x):
    lat = x[: DL // LANES * OWNED].reshape(DL // LANES, 4, 8, LANES)
    lat = lat.transpose(1, 2, 0, 3).reshape(4, 8, DL)
    rope = x[DL // LANES * OWNED :].reshape(2, 8, 2, DR).transpose(2, 0, 1, 3).reshape(4, 8, DR)
    return jnp.concatenate([lat, rope], axis=2)


def shards(queries, latent_cache, grad_output, query_blocks, key_blocks):
    core, y, zl, x = (lax.axis_index(a) for a in ("c", "y", "zl", "x"))
    row = lax.broadcasted_iota(jnp.int32, (TILE, TILE), 0)
    t = lax.broadcasted_iota(jnp.int32, (TILE, TILE), 1)
    half, t = t >> 7, t & 127
    pick = (row == (t >> 3) * 16 + (core ^ half) * 8 + (t & 7)).astype(BF)
    here = lax.dot_general(
        latent_cache, pick, (((0,), (0,)), ((), ())), preferred_element_type=F32
    ).astype(BF)
    here = jnp.concatenate([here[:, :HALF], here[:, HALF:]], axis=0)

    near = onward(here, 0)
    slant = onward(here, 1)
    singles = [
        lax.ppermute(here[:DK], "zl", [(0, 1), (1, 0)]),
        opposite(here[:DK], 0),
        opposite(here[:DK], 1),
    ]
    blocks = [here, near, swap_cores(near), slant, swap_cores(slant)]

    qt = queries.transpose(1, 2, 0)
    go = grad_output.transpose(1, 0, 2)
    place = jnp.stack([core, y, zl, x])
    early = first_part(place, query_blocks, key_blocks, qt, go, blocks)
    blocks += singles + [swap_cores(k) for k in singles]
    dqt, own, other = main_part(place, query_blocks, key_blocks, qt, blocks, early)

    other = swap_cores(other)
    sums = [own[d] + other[d].astype(F32) for d in range(4)]
    for axis in ("x", "y"):
        got = [mirrored(sums[d].astype(BF), axis, d) for d in (1, 3, 2)]
        sums = sums[0] + sum(g.astype(F32) for g in got)
    part = jnp.concatenate([unpack(sums[z]).astype(BF) for z in range(2)], axis=0)
    got = lax.all_to_all(part, ("zl", "zh"), 0, 0, tiled=True)
    return dqt.transpose(2, 0, 1), jnp.sum(got.astype(F32), axis=0)


def solution(mesh):
    fine = Mesh(mesh.devices.reshape(4, 2, 4, 4, 2), ("y", "zl", "x", "zh", "c"))
    seq, head = ("y", "zl"), ("x", "zh", "c")
    placed = (P(seq, head, None), P(seq, None), P(seq, head, None), P(), P())
    return jax.shard_map(
        shards,
        mesh=fine,
        in_specs=placed,
        out_specs=(P(seq, head, None), P(seq + head, None)),
        check_vma=False,
    )
```

```python
import functools

import jax
import jax.numpy as jnp
import numpy as np
from jax import lax
from jax.experimental import pallas as pl
from jax.experimental.pallas import tpu as pltpu
from jax.sharding import Mesh
from jax.sharding import PartitionSpec as P

H_LOC = 4
DL = 512
DR = 64
DK = 576
TILE = 256
HALF = 128
NG = 8
KEYS = NG * TILE
LOG2E = 1.4426950408889634
FLOOR = -1e30
LANES = 128
OWNED = 32
PACKED = OWNED * DK // LANES
MAIN_VMEM = 28 * 1024 * 1024
FIRST = 3
WHOLE = 5
SWAPPED = (3, 4)

softmax_scale = 0.07216878364870322

BF = jnp.bfloat16
F32 = jnp.float32


def dot(a, b):
    return lax.dot_general(a, b, (((1,), (0,)), ((), ())), preferred_element_type=F32)


def dot_nt(a, b):
    return lax.dot_general(a, b, (((1,), (1,)), ((), ())), preferred_element_type=F32)


def positions(place_ref, query_blocks_ref, key_blocks_ref):
    core, y, zl = (place_ref[n] for n in range(3))
    turn = 2 * core
    ahead = [(0 - dy) & 3 for dy in (0, 1 + turn, 1 + turn, 3 - turn, 3 - turn, 0, 2, 2)]
    floors = [zl ^ dz for dz in (0, 0, 1, 0, 1, 1, 0, 1)]
    mine = query_blocks_ref[y * 2 + zl]
    limits = []
    for up, floor in zip(ahead, floors):
        lag = (mine - key_blocks_ref[((y + up) & 3) * 2 + floor]) * TILE
        limits.append((lag - core * 8, lag - (core ^ 1) * 8))
    return ahead, floors, limits


def halves(refs):
    out = []
    for slot in range(min(WHOLE, len(refs))):
        flip = slot in SWAPPED
        blocks = [refs[slot][n * DK : (n + 1) * DK, :] for n in range(2)]
        out.append(blocks[::-1] if flip else blocks)
    rest = refs[WHOLE:]
    for slot in range(len(rest) // 2):
        out.append([rest[slot][...], rest[slot + len(rest) // 2][...]])
    return out


def offsets():
    t = lax.broadcasted_iota(jnp.int32, (HALF, TILE), 0)
    i = lax.broadcasted_iota(jnp.int32, (HALF, TILE), 1)
    return (t >> 3) * 16 + (t & 7) - i


def span(c):
    return slice(c * TILE, (c + 1) * TILE)


def weigh(keys, qt, got, delta, limits):
    scores = dot(keys, qt) * (softmax_scale * LOG2E)
    parts = [
        jnp.where(delta <= limits[b], scores[b * HALF : (b + 1) * HALF], -jnp.inf)
        for b in range(2)
    ]
    peak = jnp.maximum(*[jnp.max(p, axis=0, keepdims=True) for p in parts])
    floor = jnp.maximum(peak, FLOOR)
    e = [jnp.exp2(p - floor) for p in parts]
    total = sum(jnp.sum(p, axis=0, keepdims=True) for p in e)
    return e, dot(keys[:, :DL], got), peak, total


def first_kernel(place_ref, query_blocks_ref, key_blocks_ref, qt_ref, go_ref, *refs):
    e_ref, gp_ref, stat_ref, gl_ref, gr_ref, got_ref, k_s = refs[FIRST:]
    limits = positions(place_ref, query_blocks_ref, key_blocks_ref)[2]
    for slot, pair in enumerate(halves(refs[:FIRST])):
        for b in range(2):
            at = slot * TILE + b * HALF
            k_s[at : at + HALF, :] = pair[b].T
    delta = offsets()
    for h in range(H_LOC):
        go = go_ref[h]
        gl_ref[h * 2 * TILE : h * 2 * TILE + TILE, :] = go
        got_ref[h] = go.T
        q = qt_ref[h].T
        gl_ref[h * 2 * TILE + TILE : (h + 1) * 2 * TILE, :] = q[:, :DL]
        gr_ref[h * TILE : (h + 1) * TILE, :] = q[:, DL:]
        for c in range(FIRST):
            e, gp, peak, total = weigh(k_s[span(c), :], qt_ref[h], got_ref[h], delta, limits[c])
            for b in range(2):
                at = c * TILE + b * HALF
                e_ref[h, at : at + HALF, :] = e[b]
            gp_ref[h, span(c), :] = gp
            stat_ref[0, h, c : c + 1, :] = peak
            stat_ref[1, h, c : c + 1, :] = total


def main_kernel(place_ref, query_blocks_ref, key_blocks_ref, qt_ref, *refs):
    k_refs, refs = refs[: 2 * NG - WHOLE], refs[2 * NG - WHOLE :]
    e1_ref, gp1_ref, stat_ref, gl_ref, gr_ref, got_ref = refs[:6]
    dqt_ref, own_ref, other_ref, kt_s, k_s, e_s, gp_s, w_s = refs[6:]
    ahead, floors, limits = positions(place_ref, query_blocks_ref, key_blocks_ref)
    core, x = place_ref[0], place_ref[3]
    for slot, pair in enumerate(halves(k_refs)):
        for b in range(2):
            at = slot * TILE + b * HALF
            kt_s[:, at : at + HALF] = pair[b]
            if slot >= FIRST:
                at -= FIRST * TILE
                k_s[at : at + HALF, :] = pair[b].T
    delta = offsets()
    peaks = [[stat_ref[0, h, c : c + 1, :] for c in range(FIRST)] for h in range(H_LOC)]
    sums = [[stat_ref[1, h, c : c + 1, :] for c in range(FIRST)] for h in range(H_LOC)]
    factors = [None] * H_LOC
    corrs = [None] * H_LOC

    def load(h, c):
        if c < FIRST:
            return e1_ref[h, span(c), :], gp1_ref[h, span(c), :]
        return e_s[h, span(c - FIRST), :], gp_s[h, span(c - FIRST), :]

    def settle(h):
        peak = functools.reduce(jnp.maximum, peaks[h])
        shares = [jnp.exp2(p - peak) for p in peaks[h]]
        inv = 1.0 / sum(f * s for f, s in zip(shares, sums[h]))
        factors[h] = [f * inv for f in shares]
        corrs[h] = jnp.zeros((1, TILE), F32)

    def correct(h, c):
        e, gp = load(h, c)
        pb = (e * factors[h][c]).astype(BF)
        w_s[span(c), h * 2 * TILE : h * 2 * TILE + TILE] = pb
        corrs[h] = corrs[h] + jnp.sum(pb.astype(F32) * gp, axis=0, keepdims=True)

    def differ(h, c):
        e, gp = load(h, c)
        ds = (e * (factors[h][c] * softmax_scale) * (gp - corrs[h])).astype(BF)
        w_s[span(c), h * 2 * TILE + TILE : (h + 1) * 2 * TILE] = ds

    def to_queries(h):
        for r in range(2):
            rows = slice(r * DK // 2, (r + 1) * DK // 2)
            out = dot(kt_s[rows, :], w_s[:, h * 2 * TILE + TILE : (h + 1) * 2 * TILE])
            dqt_ref[h, rows, :] = out.astype(BF)

    def to_keys(c):
        w = w_s[span(c), :]
        lat = dot(w, gl_ref[...])
        wr = jnp.concatenate(
            [w[:, (2 * h + 1) * TILE : (2 * h + 2) * TILE] for h in range(H_LOC)], axis=1
        )
        rope = dot(wr, gr_ref[...])
        for b, ref in enumerate((own_ref, other_ref)):
            later = core ^ b
            for to in range(4):
                at = b * HALF + to * OWNED
                right = (to - x) & 3
                i = jnp.where(later == 0, right, ahead[c])
                j = jnp.where(later == 0, ahead[c], right)
                for n in range(DL // LANES):
                    ref[i, j, floors[c], n * OWNED : (n + 1) * OWNED, :] = lat[
                        at : at + OWNED, n * LANES : (n + 1) * LANES
                    ].astype(ref.dtype)
                both = jnp.concatenate(
                    [rope[at : at + OWNED // 2], rope[at + OWNED // 2 : at + OWNED]], axis=1
                )
                ref[i, j, floors[c], DL // LANES * OWNED :, :] = both.astype(ref.dtype)

    for step in range(H_LOC + 2):
        if 1 <= step <= H_LOC:
            settle(step - 1)
        for c in range(NG):
            if step < H_LOC and c >= FIRST:
                e, gp, peak, total = weigh(
                    k_s[span(c - FIRST), :], qt_ref[step], got_ref[step], delta, limits[c]
                )
                for b in range(2):
                    at = (c - FIRST) * TILE + b * HALF
                    e_s[step, at : at + HALF, :] = e[b]
                gp_s[step, span(c - FIRST), :] = gp
                peaks[step].append(peak)
                sums[step].append(total)
            if 1 <= step <= H_LOC:
                correct(step - 1, c)
            if step >= 2:
                differ(step - 2, c)
        if step >= 2:
            to_queries(step - 2)
    for c in range(NG):
        to_keys(c)


VMEM = pl.BlockSpec(memory_space=pltpu.VMEM)
SMEM = pl.BlockSpec(memory_space=pltpu.SMEM)


def first_part(place, query_blocks, key_blocks, qt, go, k_blocks):
    shapes = [
        ((H_LOC, FIRST * TILE, TILE), F32),
        ((H_LOC, FIRST * TILE, TILE), F32),
        ((2, H_LOC, 8, TILE), F32),
        ((H_LOC * 2 * TILE, DL), BF),
        ((H_LOC * TILE, DR), BF),
        ((H_LOC, DL, TILE), BF),
    ]
    return pl.pallas_call(
        first_kernel,
        in_specs=[SMEM] * 3 + [VMEM] * (2 + FIRST),
        out_specs=[VMEM] * len(shapes),
        out_shape=[jax.ShapeDtypeStruct(*s) for s in shapes],
        scratch_shapes=[pltpu.VMEM((FIRST * TILE, DK), BF)],
        cost_estimate=pl.CostEstimate(
            flops=2 * 1024 * FIRST * TILE * (DK + DL), bytes_accessed=20_000_000, transcendentals=0
        ),
        compiler_params=pltpu.CompilerParams(vmem_limit_bytes=24 * 1024 * 1024),
    )(place, query_blocks, key_blocks, qt, go, *k_blocks)


def main_part(place, query_blocks, key_blocks, qt, k_blocks, early):
    rest = (NG - FIRST) * TILE
    return pl.pallas_call(
        main_kernel,
        in_specs=[SMEM] * 3 + [VMEM] * (1 + len(k_blocks) + len(early)),
        out_specs=[VMEM] * 3,
        out_shape=[
            jax.ShapeDtypeStruct((H_LOC, DK, TILE), BF),
            jax.ShapeDtypeStruct((4, 4, 2, PACKED, LANES), F32),
            jax.ShapeDtypeStruct((4, 4, 2, PACKED, LANES), BF),
        ],
        scratch_shapes=[
            pltpu.VMEM((DK, KEYS), BF),
            pltpu.VMEM((rest, DK), BF),
            pltpu.VMEM((H_LOC, rest, TILE), F32),
            pltpu.VMEM((H_LOC, rest, TILE), F32),
            pltpu.VMEM((KEYS, H_LOC * 2 * TILE), BF),
        ],
        compiler_params=pltpu.CompilerParams(vmem_limit_bytes=MAIN_VMEM),
    )(place, query_blocks, key_blocks, qt, *k_blocks, *early)


def swap_cores(x):
    return lax.ppermute(x, "c", [(0, 1), (1, 0)])


def onward(x, dz):
    pairs = [
        ((y * 2 + z) * 2 + c, ((y + 1 - 2 * c) % 4 * 2 + (z ^ dz)) * 2 + c)
        for y in range(4)
        for z in range(2)
        for c in range(2)
    ]
    return lax.ppermute(x, ("y", "zl", "c"), pairs)


def crossed(x, first, step):
    def target(n):
        y, x, c = n // 8, n // 2 % 4, n % 2
        if (c == 0) == first:
            x = (x + step) % 4
        else:
            y = (y + step) % 4
        return (y * 4 + x) * 2 + c

    return lax.ppermute(x, ("y", "x", "c"), [(n, target(n)) for n in range(32)])


def opposite(x, dz):
    pairs = [(y * 2 + z, (y + 2) % 4 * 2 + (z ^ dz)) for y in range(4) for z in range(2)]
    return lax.ppermute(x, ("y", "zl"), pairs)


def unpack(x):
    lat = x[: DL // LANES * OWNED].reshape(DL // LANES, 4, 8, LANES)
    lat = lat.transpose(1, 2, 0, 3).reshape(4, 8, DL)
    rope = x[DL // LANES * OWNED :].reshape(2, 8, 2, DR).transpose(2, 0, 1, 3).reshape(4, 8, DR)
    return jnp.concatenate([lat, rope], axis=2)


def shards(queries, latent_cache, grad_output, query_blocks, key_blocks):
    core, y, zl, x = (lax.axis_index(a) for a in ("c", "y", "zl", "x"))
    row = lax.broadcasted_iota(jnp.int32, (TILE, TILE), 0)
    t = lax.broadcasted_iota(jnp.int32, (TILE, TILE), 1)
    half, t = t >> 7, t & 127
    pick = (row == (t >> 3) * 16 + (core ^ half) * 8 + (t & 7)).astype(BF)
    here = lax.dot_general(
        latent_cache, pick, (((0,), (0,)), ((), ())), preferred_element_type=F32
    ).astype(BF)
    here = jnp.concatenate([here[:, :HALF], here[:, HALF:]], axis=0)

    near = onward(here, 0)
    slant = onward(here, 1)
    singles = [
        lax.ppermute(here[:DK], "zl", [(0, 1), (1, 0)]),
        opposite(here[:DK], 0),
        opposite(here[:DK], 1),
    ]

    qt = queries.transpose(1, 2, 0)
    go = grad_output.transpose(1, 0, 2)
    go, near, slant, *singles = lax.optimization_barrier((go, near, slant, *singles))
    blocks = [here, near, slant]
    place = jnp.stack([core, y, zl, x])
    early = first_part(place, query_blocks, key_blocks, qt, go, blocks)
    blocks += [swap_cores(near), swap_cores(slant)] + singles + [swap_cores(k) for k in singles]
    dqt, own, other = main_part(place, query_blocks, key_blocks, qt, blocks, early)

    other = swap_cores(other)
    sums = [own[d] + other[d].astype(F32) for d in range(4)]
    for first in (True, False):
        got = [crossed(sums[d].astype(BF), first, d) for d in (2, 1, 3)]
        sums = sums[0] + sum(g.astype(F32) for g in got)
    part = jnp.concatenate([unpack(sums[z]).astype(BF) for z in range(2)], axis=0)
    got = lax.all_to_all(part, ("zl", "zh"), 0, 0, tiled=True)
    return dqt.transpose(2, 0, 1), jnp.sum(got.astype(F32), axis=0)


def solution(mesh):
    fine = Mesh(mesh.devices.reshape(4, 2, 4, 4, 2), ("y", "zl", "x", "zh", "c"))
    seq, head = ("y", "zl"), ("x", "zh", "c")
    placed = (P(seq, head, None), P(seq, None), P(seq, head, None), P(), P())
    return jax.shard_map(
        shards,
        mesh=fine,
        in_specs=placed,
        out_specs=(P(seq, head, None), P(seq + head, None)),
        check_vma=False,
    )
```

```python
import functools

import jax
import jax.numpy as jnp
import numpy as np
from jax import lax
from jax.experimental import pallas as pl
from jax.experimental.pallas import tpu as pltpu
from jax.sharding import Mesh
from jax.sharding import PartitionSpec as P

H_LOC = 4
DL = 512
DR = 64
DK = 576
TILE = 256
HALF = 128
NG = 8
KEYS = NG * TILE
LOG2E = 1.4426950408889634
FLOOR = -1e30
LANES = 128
OWNED = 32
PACKED = OWNED * DK // LANES
MAIN_VMEM = 28 * 1024 * 1024
FIRST = 3
WHOLE = 5
SWAPPED = (3, 4)

softmax_scale = 0.07216878364870322

BF = jnp.bfloat16
F32 = jnp.float32


def dot(a, b):
    return lax.dot_general(a, b, (((1,), (0,)), ((), ())), preferred_element_type=F32)


def dot_nt(a, b):
    return lax.dot_general(a, b, (((1,), (1,)), ((), ())), preferred_element_type=F32)


def positions(place_ref):
    core, y, zl = (place_ref[n] for n in range(3))
    turn = 2 * core
    ahead = [(0 - dy) & 3 for dy in (0, 1 + turn, 1 + turn, 3 - turn, 3 - turn, 0, 2, 2)]
    floors = [zl ^ dz for dz in (0, 0, 1, 0, 1, 1, 0, 1)]
    mine = place_ref[4 + y * 2 + zl]
    limits = []
    for up, floor in zip(ahead, floors):
        lag = (mine - place_ref[4 + NG + ((y + up) & 3) * 2 + floor]) * TILE
        limits.append((lag - core * 8, lag - (core ^ 1) * 8))
    return ahead, floors, limits


def halves(refs):
    out = []
    for slot in range(min(WHOLE, len(refs))):
        flip = slot in SWAPPED
        blocks = [refs[slot][n * DK : (n + 1) * DK, :] for n in range(2)]
        out.append(blocks[::-1] if flip else blocks)
    rest = refs[WHOLE:]
    for slot in range(len(rest) // 2):
        out.append([rest[slot][...], rest[slot + len(rest) // 2][...]])
    return out


def offsets():
    t = lax.broadcasted_iota(jnp.int32, (HALF, TILE), 0)
    i = lax.broadcasted_iota(jnp.int32, (HALF, TILE), 1)
    return (t >> 3) * 16 + (t & 7) - i


def span(c):
    return slice(c * TILE, (c + 1) * TILE)


def weigh(keys, qt, got, delta, limits):
    scores = dot(keys, qt) * (softmax_scale * LOG2E)
    parts = [
        jnp.where(delta <= limits[b], scores[b * HALF : (b + 1) * HALF], -jnp.inf)
        for b in range(2)
    ]
    peak = jnp.maximum(*[jnp.max(p, axis=0, keepdims=True) for p in parts])
    floor = jnp.maximum(peak, FLOOR)
    e = [jnp.exp2(p - floor) for p in parts]
    total = sum(jnp.sum(p, axis=0, keepdims=True) for p in e)
    return e, dot(keys[:, :DL], got), peak, total


def first_kernel(place_ref, qt_ref, go_ref, *refs):
    e_ref, gp_ref, stat_ref, gl_ref, gr_ref, got_ref, k_s = refs[FIRST:]
    limits = positions(place_ref)[2]
    for slot, pair in enumerate(halves(refs[:FIRST])):
        for b in range(2):
            at = slot * TILE + b * HALF
            k_s[at : at + HALF, :] = pair[b].T
    delta = offsets()
    for h in range(H_LOC):
        go = go_ref[h]
        gl_ref[h * 2 * TILE : h * 2 * TILE + TILE, :] = go
        got_ref[h] = go.T
        q = qt_ref[h].T
        gl_ref[h * 2 * TILE + TILE : (h + 1) * 2 * TILE, :] = q[:, :DL]
        gr_ref[h * TILE : (h + 1) * TILE, :] = q[:, DL:]
        for c in range(FIRST):
            e, gp, peak, total = weigh(k_s[span(c), :], qt_ref[h], got_ref[h], delta, limits[c])
            for b in range(2):
                at = c * TILE + b * HALF
                e_ref[h, at : at + HALF, :] = e[b]
            gp_ref[h, span(c), :] = gp
            stat_ref[0, h, c : c + 1, :] = peak
            stat_ref[1, h, c : c + 1, :] = total


def to_keys(place_ref, half, w_ref, gl_ref, gr_ref, ref):
    ahead, floors, _ = positions(place_ref)
    core, x = place_ref[0], place_ref[3]
    later = core ^ half
    for c in range(NG // 2):
        w = w_ref[span(c), :]
        lat = dot(w, gl_ref[...])
        wr = jnp.concatenate(
            [w[:, (2 * h + 1) * TILE : (2 * h + 2) * TILE] for h in range(H_LOC)], axis=1
        )
        rope = dot(wr, gr_ref[...])
        for b in range(2):
            slot = 2 * c + b
            for to in range(4):
                at = b * HALF + to * OWNED
                right = (to - x) & 3
                i = jnp.where(later == 0, right, ahead[slot])
                j = jnp.where(later == 0, ahead[slot], right)
                for n in range(DL // LANES):
                    ref[i, j, floors[slot], n * OWNED : (n + 1) * OWNED, :] = lat[
                        at : at + OWNED, n * LANES : (n + 1) * LANES
                    ].astype(ref.dtype)
                both = jnp.concatenate(
                    [rope[at : at + OWNED // 2], rope[at + OWNED // 2 : at + OWNED]], axis=1
                )
                ref[i, j, floors[slot], DL // LANES * OWNED :, :] = both.astype(ref.dtype)


def main_kernel(place_ref, qt_ref, *refs):
    k_refs, refs = refs[: 2 * NG - WHOLE], refs[2 * NG - WHOLE :]
    e1_ref, gp1_ref, stat_ref, gl_ref, gr_ref, got_ref = refs[:6]
    dqt_ref, own_w_ref, other_ref, kt_s, k_s, e_s, gp_s, other_w_s = refs[6:]
    limits = positions(place_ref)[2]
    w_refs = (own_w_ref, other_w_s)
    for slot, pair in enumerate(halves(k_refs)):
        for b in range(2):
            at = b * KEYS // 2 + slot * HALF
            kt_s[:, at : at + HALF] = pair[b]
            if slot >= FIRST:
                at = (slot - FIRST) * TILE + b * HALF
                k_s[at : at + HALF, :] = pair[b].T
    delta = offsets()
    peaks = [[stat_ref[0, h, c : c + 1, :] for c in range(FIRST)] for h in range(H_LOC)]
    sums = [[stat_ref[1, h, c : c + 1, :] for c in range(FIRST)] for h in range(H_LOC)]
    factors = [None] * H_LOC
    corrs = [None] * H_LOC

    def load(h, c):
        if c < FIRST:
            return e1_ref[h, span(c), :], gp1_ref[h, span(c), :]
        return e_s[h, span(c - FIRST), :], gp_s[h, span(c - FIRST), :]

    def keep(h, c, kind, value):
        at = (2 * h + kind) * TILE
        for b, ref in enumerate(w_refs):
            ref[c * HALF : (c + 1) * HALF, at : at + TILE] = value[b * HALF : (b + 1) * HALF]

    def settle(h):
        peak = functools.reduce(jnp.maximum, peaks[h])
        shares = [jnp.exp2(p - peak) for p in peaks[h]]
        inv = 1.0 / sum(f * s for f, s in zip(shares, sums[h]))
        factors[h] = [f * inv for f in shares]
        corrs[h] = jnp.zeros((1, TILE), F32)

    def correct(h, c):
        e, gp = load(h, c)
        pb = (e * factors[h][c]).astype(BF)
        keep(h, c, 0, pb)
        corrs[h] = corrs[h] + jnp.sum(pb.astype(F32) * gp, axis=0, keepdims=True)

    def differ(h, c):
        e, gp = load(h, c)
        ds = (e * (factors[h][c] * softmax_scale) * (gp - corrs[h])).astype(BF)
        keep(h, c, 1, ds)

    def to_queries(h):
        for r in range(2):
            rows = slice(r * DK // 2, (r + 1) * DK // 2)
            at = (2 * h + 1) * TILE
            out = dot(kt_s[rows, : KEYS // 2], own_w_ref[:, at : at + TILE])
            out = out + dot(kt_s[rows, KEYS // 2 :], other_w_s[:, at : at + TILE])
            dqt_ref[h, rows, :] = out.astype(BF)

    for step in range(H_LOC + 2):
        if 1 <= step <= H_LOC:
            settle(step - 1)
        for c in range(NG):
            if step < H_LOC and c >= FIRST:
                e, gp, peak, total = weigh(
                    k_s[span(c - FIRST), :], qt_ref[step], got_ref[step], delta, limits[c]
                )
                for b in range(2):
                    at = (c - FIRST) * TILE + b * HALF
                    e_s[step, at : at + HALF, :] = e[b]
                gp_s[step, span(c - FIRST), :] = gp
                peaks[step].append(peak)
                sums[step].append(total)
            if 1 <= step <= H_LOC:
                correct(step - 1, c)
            if step >= 2:
                differ(step - 2, c)
        if step >= 2:
            to_queries(step - 2)
    to_keys(place_ref, 1, other_w_s, gl_ref, gr_ref, other_ref)


def own_kernel(place_ref, w_ref, gl_ref, gr_ref, own_ref):
    to_keys(place_ref, 0, w_ref, gl_ref, gr_ref, own_ref)


VMEM = pl.BlockSpec(memory_space=pltpu.VMEM)
SMEM = pl.BlockSpec(memory_space=pltpu.SMEM)


def first_part(place, qt, go, k_blocks):
    shapes = [
        ((H_LOC, FIRST * TILE, TILE), F32),
        ((H_LOC, FIRST * TILE, TILE), F32),
        ((2, H_LOC, 8, TILE), F32),
        ((H_LOC * 2 * TILE, DL), BF),
        ((H_LOC * TILE, DR), BF),
        ((H_LOC, DL, TILE), BF),
    ]
    return pl.pallas_call(
        first_kernel,
        in_specs=[SMEM] + [VMEM] * (2 + FIRST),
        out_specs=[VMEM] * len(shapes),
        out_shape=[jax.ShapeDtypeStruct(*s) for s in shapes],
        scratch_shapes=[pltpu.VMEM((FIRST * TILE, DK), BF)],
        cost_estimate=pl.CostEstimate(
            flops=2 * 1024 * FIRST * TILE * (DK + DL), bytes_accessed=20_000_000, transcendentals=0
        ),
        compiler_params=pltpu.CompilerParams(vmem_limit_bytes=24 * 1024 * 1024),
    )(place, qt, go, *k_blocks)


def main_part(place, qt, k_blocks, early):
    rest = (NG - FIRST) * TILE
    return pl.pallas_call(
        main_kernel,
        in_specs=[SMEM] + [VMEM] * (1 + len(k_blocks) + len(early)),
        out_specs=[VMEM] * 3,
        out_shape=[
            jax.ShapeDtypeStruct((H_LOC, DK, TILE), BF),
            jax.ShapeDtypeStruct((KEYS // 2, H_LOC * 2 * TILE), BF),
            jax.ShapeDtypeStruct((4, 4, 2, PACKED, LANES), BF),
        ],
        scratch_shapes=[
            pltpu.VMEM((DK, KEYS), BF),
            pltpu.VMEM((rest, DK), BF),
            pltpu.VMEM((H_LOC, rest, TILE), F32),
            pltpu.VMEM((H_LOC, rest, TILE), F32),
            pltpu.VMEM((KEYS // 2, H_LOC * 2 * TILE), BF),
        ],
        compiler_params=pltpu.CompilerParams(vmem_limit_bytes=MAIN_VMEM),
    )(place, qt, *k_blocks, *early)


def own_part(place, weights, gl, gr):
    return pl.pallas_call(
        own_kernel,
        in_specs=[SMEM] + [VMEM] * 3,
        out_specs=VMEM,
        out_shape=jax.ShapeDtypeStruct((4, 4, 2, PACKED, LANES), F32),
        cost_estimate=pl.CostEstimate(
            flops=KEYS * H_LOC * 2 * TILE * DK, bytes_accessed=9_000_000, transcendentals=0
        ),
        compiler_params=pltpu.CompilerParams(vmem_limit_bytes=16 * 1024 * 1024),
    )(place, weights, gl, gr)


def swap_cores(x):
    return lax.ppermute(x, "c", [(0, 1), (1, 0)])


def onward(x, dz):
    pairs = [
        ((y * 2 + z) * 2 + c, ((y + 1 - 2 * c) % 4 * 2 + (z ^ dz)) * 2 + c)
        for y in range(4)
        for z in range(2)
        for c in range(2)
    ]
    return lax.ppermute(x, ("y", "zl", "c"), pairs)


def crossed(x, first, step):
    def target(n):
        y, x, c = n // 8, n // 2 % 4, n % 2
        if (c == 0) == first:
            x = (x + step) % 4
        else:
            y = (y + step) % 4
        return (y * 4 + x) * 2 + c

    return lax.ppermute(x, ("y", "x", "c"), [(n, target(n)) for n in range(32)])


def opposite(x, dz):
    pairs = [(y * 2 + z, (y + 2) % 4 * 2 + (z ^ dz)) for y in range(4) for z in range(2)]
    return lax.ppermute(x, ("y", "zl"), pairs)


def unpack(x):
    lat = x[: DL // LANES * OWNED].reshape(DL // LANES, 4, 8, LANES)
    lat = lat.transpose(1, 2, 0, 3).reshape(4, 8, DL)
    rope = x[DL // LANES * OWNED :].reshape(2, 8, 2, DR).transpose(2, 0, 1, 3).reshape(4, 8, DR)
    return jnp.concatenate([lat, rope], axis=2)


def shards(queries, latent_cache, grad_output, query_blocks, key_blocks):
    core, y, zl, x = (lax.axis_index(a) for a in ("c", "y", "zl", "x"))
    row = lax.broadcasted_iota(jnp.int32, (TILE, TILE), 0)
    t = lax.broadcasted_iota(jnp.int32, (TILE, TILE), 1)
    half, t = t >> 7, t & 127
    pick = (row == (t >> 3) * 16 + (core ^ half) * 8 + (t & 7)).astype(BF)
    here = lax.dot_general(
        latent_cache, pick, (((0,), (0,)), ((), ())), preferred_element_type=F32
    ).astype(BF)
    here = jnp.concatenate([here[:, :HALF], here[:, HALF:]], axis=0)

    near = onward(here, 0)
    slant = onward(here, 1)
    singles = [
        lax.ppermute(here[:DK], "zl", [(0, 1), (1, 0)]),
        opposite(here[:DK], 0),
        opposite(here[:DK], 1),
    ]

    place = jnp.concatenate([jnp.stack([core, y, zl, x]), query_blocks, key_blocks])
    qt = queries.transpose(1, 2, 0)
    go = grad_output.transpose(1, 0, 2)
    go, place = lax.optimization_barrier((go, place))
    blocks = [here, near, slant]
    early = list(first_part(place, qt, go, blocks))
    blocks += [swap_cores(near), swap_cores(slant)]
    early[2], *singles = lax.optimization_barrier((early[2], *singles))
    blocks += singles + [swap_cores(k) for k in singles]
    dqt, weights, other = main_part(place, qt, blocks, early)
    other = swap_cores(other)
    own = own_part(place, weights, early[3], early[4])

    sums = [own[d] + other[d].astype(F32) for d in range(4)]
    for first in (True, False):
        got = [crossed(sums[d].astype(BF), first, d) for d in (2, 1, 3)]
        sums = sums[0] + sum(g.astype(F32) for g in got)
    part = jnp.concatenate([unpack(sums[z]).astype(BF) for z in range(2)], axis=0)
    got = lax.all_to_all(part, ("zl", "zh"), 0, 0, tiled=True)
    return dqt.transpose(2, 0, 1), jnp.sum(got.astype(F32), axis=0)


def solution(mesh):
    fine = Mesh(mesh.devices.reshape(4, 2, 4, 4, 2), ("y", "zl", "x", "zh", "c"))
    seq, head = ("y", "zl"), ("x", "zh", "c")
    placed = (P(seq, head, None), P(seq, None), P(seq, head, None), P(), P())
    return jax.shard_map(
        shards,
        mesh=fine,
        in_specs=placed,
        out_specs=(P(seq, head, None), P(seq + head, None)),
        check_vma=False,
    )
```

```python
import functools

import jax
import jax.numpy as jnp
import numpy as np
from jax import lax
from jax.experimental import pallas as pl
from jax.experimental.pallas import tpu as pltpu
from jax.sharding import Mesh
from jax.sharding import PartitionSpec as P

H_LOC = 4
DL = 512
DR = 64
DK = 576
TILE = 256
HALF = 128
NG = 8
KEYS = NG * TILE
LOG2E = 1.4426950408889634
FLOOR = -1e30
LANES = 128
OWNED = 32
PACKED = OWNED * DK // LANES
MAIN_VMEM = 23 * 1024 * 1024
FIRST = 3
WHOLE = 5
SWAPPED = (3, 4)

softmax_scale = 0.07216878364870322

BF = jnp.bfloat16
F32 = jnp.float32


def dot(a, b):
    return lax.dot_general(a, b, (((1,), (0,)), ((), ())), preferred_element_type=F32)


def dot_nt(a, b):
    return lax.dot_general(a, b, (((1,), (1,)), ((), ())), preferred_element_type=F32)


def directions(place_ref):
    core, zl = place_ref[0], place_ref[2]
    turn = 2 * core
    ahead = [(0 - dy) & 3 for dy in (0, 1 + turn, 1 + turn, 3 - turn, 3 - turn, 0, 2, 2)]
    floors = [zl ^ dz for dz in (0, 0, 1, 0, 1, 1, 0, 1)]
    return ahead, floors


def positions(place_ref, query_blocks_ref, key_blocks_ref):
    core, y, zl = (place_ref[n] for n in range(3))
    ahead, floors = directions(place_ref)
    mine = query_blocks_ref[y * 2 + zl]
    limits = []
    for up, floor in zip(ahead, floors):
        lag = (mine - key_blocks_ref[((y + up) & 3) * 2 + floor]) * TILE
        limits.append((lag - core * 8, lag - (core ^ 1) * 8))
    return limits


def halves(refs):
    out = []
    for slot in range(min(WHOLE, len(refs))):
        flip = slot in SWAPPED
        blocks = [refs[slot][n * DK : (n + 1) * DK, :] for n in range(2)]
        out.append(blocks[::-1] if flip else blocks)
    rest = refs[WHOLE:]
    for slot in range(len(rest) // 2):
        out.append([rest[slot][...], rest[slot + len(rest) // 2][...]])
    return out


def offsets():
    t = lax.broadcasted_iota(jnp.int32, (HALF, TILE), 0)
    i = lax.broadcasted_iota(jnp.int32, (HALF, TILE), 1)
    return (t >> 3) * 16 + (t & 7) - i


def span(c):
    return slice(c * TILE, (c + 1) * TILE)


def weigh(keys, qt, got, delta, limits):
    scores = dot(keys, qt) * (softmax_scale * LOG2E)
    parts = [
        jnp.where(delta <= limits[b], scores[b * HALF : (b + 1) * HALF], -jnp.inf)
        for b in range(2)
    ]
    peak = jnp.maximum(*[jnp.max(p, axis=0, keepdims=True) for p in parts])
    floor = jnp.maximum(peak, FLOOR)
    e = [jnp.exp2(p - floor) for p in parts]
    total = sum(jnp.sum(p, axis=0, keepdims=True) for p in e)
    return e, dot(keys[:, :DL], got), peak, total


def first_kernel(place_ref, query_blocks_ref, key_blocks_ref, qt_ref, go_ref, *refs):
    e_ref, gp_ref, stat_ref, gl_ref, gr_ref, got_ref, k_s = refs[FIRST:]
    limits = positions(place_ref, query_blocks_ref, key_blocks_ref)
    for slot, pair in enumerate(halves(refs[:FIRST])):
        for b in range(2):
            at = slot * TILE + b * HALF
            k_s[at : at + HALF, :] = pair[b].T
    delta = offsets()
    for h in range(H_LOC):
        go = go_ref[h]
        gl_ref[h * 2 * TILE : h * 2 * TILE + TILE, :] = go
        got_ref[h] = go.T
        q = qt_ref[h].T
        gl_ref[h * 2 * TILE + TILE : (h + 1) * 2 * TILE, :] = q[:, :DL]
        gr_ref[h * TILE : (h + 1) * TILE, :] = q[:, DL:]
        for c in range(FIRST):
            e, gp, peak, total = weigh(k_s[span(c), :], qt_ref[h], got_ref[h], delta, limits[c])
            for b in range(2):
                at = c * TILE + b * HALF
                e_ref[h, at : at + HALF, :] = e[b]
            gp_ref[h, span(c), :] = gp
            stat_ref[0, h, c : c + 1, :] = peak
            stat_ref[1, h, c : c + 1, :] = total


def to_keys(place_ref, half, w_ref, gl_ref, gr_ref, ref):
    ahead, floors = directions(place_ref)
    core, x = place_ref[0], place_ref[3]
    later = core ^ half
    for c in range(NG // 2):
        w = w_ref[span(c), :]
        lat = dot(w, gl_ref[...])
        wr = jnp.concatenate(
            [w[:, (2 * h + 1) * TILE : (2 * h + 2) * TILE] for h in range(H_LOC)], axis=1
        )
        rope = dot(wr, gr_ref[...])
        for b in range(2):
            slot = 2 * c + b
            for to in range(4):
                at = b * HALF + to * OWNED
                right = (to - x) & 3
                i = jnp.where(later == 0, right, ahead[slot])
                j = jnp.where(later == 0, ahead[slot], right)
                for n in range(DL // LANES):
                    ref[i, j, floors[slot], n * OWNED : (n + 1) * OWNED, :] = lat[
                        at : at + OWNED, n * LANES : (n + 1) * LANES
                    ].astype(ref.dtype)
                both = jnp.concatenate(
                    [rope[at : at + OWNED // 2], rope[at + OWNED // 2 : at + OWNED]], axis=1
                )
                ref[i, j, floors[slot], DL // LANES * OWNED :, :] = both.astype(ref.dtype)


def main_kernel(place_ref, query_blocks_ref, key_blocks_ref, qt_ref, *refs):
    k_refs, refs = refs[: 2 * NG - WHOLE], refs[2 * NG - WHOLE :]
    e1_ref, gp1_ref, stat_ref, gl_ref, gr_ref, got_ref = refs[:6]
    dqt_ref, own_w_ref, other_ref, kt_s, k_s, e_s, gp_s, other_w_s = refs[6:]
    limits = positions(place_ref, query_blocks_ref, key_blocks_ref)
    w_refs = (own_w_ref, other_w_s)
    for slot, pair in enumerate(halves(k_refs)):
        for b in range(2):
            at = b * KEYS // 2 + slot * HALF
            kt_s[:, at : at + HALF] = pair[b]
            if slot >= FIRST:
                at = (slot - FIRST) * TILE + b * HALF
                k_s[at : at + HALF, :] = pair[b].T
    delta = offsets()
    peaks = [[stat_ref[0, h, c : c + 1, :] for c in range(FIRST)] for h in range(H_LOC)]
    sums = [[stat_ref[1, h, c : c + 1, :] for c in range(FIRST)] for h in range(H_LOC)]
    factors = [None] * H_LOC
    corrs = [None] * H_LOC

    def load(h, c):
        if c < FIRST:
            return e1_ref[h, span(c), :], gp1_ref[h, span(c), :]
        return e_s[h, span(c - FIRST), :], gp_s[h, span(c - FIRST), :]

    def keep(h, c, kind, value):
        at = (2 * h + kind) * TILE
        for b, ref in enumerate(w_refs):
            ref[c * HALF : (c + 1) * HALF, at : at + TILE] = value[b * HALF : (b + 1) * HALF]

    def settle(h):
        peak = functools.reduce(jnp.maximum, peaks[h])
        shares = [jnp.exp2(p - peak) for p in peaks[h]]
        inv = 1.0 / sum(f * s for f, s in zip(shares, sums[h]))
        factors[h] = [f * inv for f in shares]
        corrs[h] = jnp.zeros((1, TILE), F32)

    def correct(h, c):
        e, gp = load(h, c)
        pb = (e * factors[h][c]).astype(BF)
        keep(h, c, 0, pb)
        corrs[h] = corrs[h] + jnp.sum(pb.astype(F32) * gp, axis=0, keepdims=True)

    def differ(h, c):
        e, gp = load(h, c)
        ds = (e * (factors[h][c] * softmax_scale) * (gp - corrs[h])).astype(BF)
        keep(h, c, 1, ds)

    def to_queries(h):
        for r in range(2):
            rows = slice(r * DK // 2, (r + 1) * DK // 2)
            at = (2 * h + 1) * TILE
            out = dot(kt_s[rows, : KEYS // 2], own_w_ref[:, at : at + TILE])
            out = out + dot(kt_s[rows, KEYS // 2 :], other_w_s[:, at : at + TILE])
            dqt_ref[h, rows, :] = out.astype(BF)

    for step in range(H_LOC + 2):
        if 1 <= step <= H_LOC:
            settle(step - 1)
        for c in range(NG):
            if step < H_LOC and c >= FIRST:
                e, gp, peak, total = weigh(
                    k_s[span(c - FIRST), :], qt_ref[step], got_ref[step], delta, limits[c]
                )
                for b in range(2):
                    at = (c - FIRST) * TILE + b * HALF
                    e_s[step, at : at + HALF, :] = e[b]
                gp_s[step, span(c - FIRST), :] = gp
                peaks[step].append(peak)
                sums[step].append(total)
            if 1 <= step <= H_LOC:
                correct(step - 1, c)
            if step >= 2:
                differ(step - 2, c)
        if step >= 2:
            to_queries(step - 2)
    to_keys(place_ref, 1, other_w_s, gl_ref, gr_ref, other_ref)


def own_kernel(place_ref, w_ref, gl_ref, gr_ref, own_ref):
    to_keys(place_ref, 0, w_ref, gl_ref, gr_ref, own_ref)


VMEM = pl.BlockSpec(memory_space=pltpu.VMEM)
SMEM = pl.BlockSpec(memory_space=pltpu.SMEM)


def first_part(place, query_blocks, key_blocks, qt, go, k_blocks):
    shapes = [
        ((H_LOC, FIRST * TILE, TILE), F32),
        ((H_LOC, FIRST * TILE, TILE), F32),
        ((2, H_LOC, 8, TILE), F32),
        ((H_LOC * 2 * TILE, DL), BF),
        ((H_LOC * TILE, DR), BF),
        ((H_LOC, DL, TILE), BF),
    ]
    return pl.pallas_call(
        first_kernel,
        in_specs=[SMEM] * 3 + [VMEM] * (2 + FIRST),
        out_specs=[VMEM] * len(shapes),
        out_shape=[jax.ShapeDtypeStruct(*s) for s in shapes],
        scratch_shapes=[pltpu.VMEM((FIRST * TILE, DK), BF)],
        cost_estimate=pl.CostEstimate(
            flops=2 * 1024 * FIRST * TILE * (DK + DL), bytes_accessed=20_000_000, transcendentals=0
        ),
        compiler_params=pltpu.CompilerParams(vmem_limit_bytes=16 * 1024 * 1024),
    )(place, query_blocks, key_blocks, qt, go, *k_blocks)


def main_part(place, query_blocks, key_blocks, qt, k_blocks, early):
    rest = (NG - FIRST) * TILE
    return pl.pallas_call(
        main_kernel,
        in_specs=[SMEM] * 3 + [VMEM] * (1 + len(k_blocks) + len(early)),
        out_specs=[VMEM] * 3,
        out_shape=[
            jax.ShapeDtypeStruct((H_LOC, DK, TILE), BF),
            jax.ShapeDtypeStruct((KEYS // 2, H_LOC * 2 * TILE), BF),
            jax.ShapeDtypeStruct((4, 4, 2, PACKED, LANES), BF),
        ],
        scratch_shapes=[
            pltpu.VMEM((DK, KEYS), BF),
            pltpu.VMEM((rest, DK), BF),
            pltpu.VMEM((H_LOC, rest, TILE), F32),
            pltpu.VMEM((H_LOC, rest, TILE), F32),
            pltpu.VMEM((KEYS // 2, H_LOC * 2 * TILE), BF),
        ],
        compiler_params=pltpu.CompilerParams(vmem_limit_bytes=MAIN_VMEM),
    )(place, query_blocks, key_blocks, qt, *k_blocks, *early)


def own_part(place, weights, gl, gr):
    return pl.pallas_call(
        own_kernel,
        in_specs=[SMEM] + [VMEM] * 3,
        out_specs=VMEM,
        out_shape=jax.ShapeDtypeStruct((4, 4, 2, PACKED, LANES), F32),
        cost_estimate=pl.CostEstimate(
            flops=KEYS * H_LOC * 2 * TILE * DK, bytes_accessed=9_000_000, transcendentals=0
        ),
        compiler_params=pltpu.CompilerParams(vmem_limit_bytes=12 * 1024 * 1024),
    )(place, weights, gl, gr)


def swap_cores(x):
    return lax.ppermute(x, "c", [(0, 1), (1, 0)])


def onward(x, dz):
    pairs = [
        ((y * 2 + z) * 2 + c, ((y + 1 - 2 * c) % 4 * 2 + (z ^ dz)) * 2 + c)
        for y in range(4)
        for z in range(2)
        for c in range(2)
    ]
    return lax.ppermute(x, ("y", "zl", "c"), pairs)


def crossed(x, first, step):
    def target(n):
        y, x, c = n // 8, n // 2 % 4, n % 2
        if (c == 0) == first:
            x = (x + step) % 4
        else:
            y = (y + step) % 4
        return (y * 4 + x) * 2 + c

    return lax.ppermute(x, ("y", "x", "c"), [(n, target(n)) for n in range(32)])


def unpack(x):
    lat = x[: DL // LANES * OWNED].reshape(DL // LANES, 4, 8, LANES)
    lat = lat.transpose(1, 2, 0, 3).reshape(4, 8, DL)
    rope = x[DL // LANES * OWNED :].reshape(2, 8, 2, DR).transpose(2, 0, 1, 3).reshape(4, 8, DR)
    return jnp.concatenate([lat, rope], axis=2)


def shards(queries, latent_cache, grad_output, query_blocks, key_blocks):
    core, y, zl, x = (lax.axis_index(a) for a in ("c", "y", "zl", "x"))
    row = lax.broadcasted_iota(jnp.int32, (TILE, TILE), 0)
    t = lax.broadcasted_iota(jnp.int32, (TILE, TILE), 1)
    half, t = t >> 7, t & 127
    pick = (row == (t >> 3) * 16 + (core ^ half) * 8 + (t & 7)).astype(BF)
    here = lax.dot_general(
        latent_cache, pick, (((0,), (0,)), ((), ())), preferred_element_type=F32
    ).astype(BF)
    here = jnp.concatenate([here[:, :HALF], here[:, HALF:]], axis=0)

    near = onward(here, 0)
    slant = onward(here, 1)
    beside = lax.ppermute(here[:DK], "zl", [(0, 1), (1, 0)])

    place = jnp.stack([core, y, zl, x])
    qt = queries.transpose(1, 2, 0)
    go = grad_output.transpose(1, 0, 2)
    go, near, slant = lax.optimization_barrier((go, near, slant))
    singles = [beside, onward(near[:DK], 0), onward(slant[:DK], 0)]
    swapped = [swap_cores(near), swap_cores(slant)]
    early = list(first_part(place, query_blocks, key_blocks, qt, go, [here, near, slant]))
    early[2], *singles = lax.optimization_barrier((early[2], *singles))
    blocks = [here, near, slant] + swapped + singles + [swap_cores(k) for k in singles]
    dqt, weights, other = main_part(place, query_blocks, key_blocks, qt, blocks, early)
    other = swap_cores(other)
    own = own_part(place, weights, early[3], early[4])

    sums = [own[d] + other[d].astype(F32) for d in range(4)]
    for first in (True, False):
        got = [crossed(sums[d].astype(BF), first, d) for d in (2, 1, 3)]
        sums = sums[0] + sum(g.astype(F32) for g in got)
    part = jnp.concatenate([unpack(sums[z]).astype(BF) for z in range(2)], axis=0)
    got = lax.all_to_all(part, ("zl", "zh"), 0, 0, tiled=True)
    return dqt.transpose(2, 0, 1), jnp.sum(got.astype(F32), axis=0)


def solution(mesh):
    fine = Mesh(mesh.devices.reshape(4, 2, 4, 4, 2), ("y", "zl", "x", "zh", "c"))
    seq, head = ("y", "zl"), ("x", "zh", "c")
    placed = (P(seq, head, None), P(seq, None), P(seq, head, None), P(), P())
    return jax.shard_map(
        shards,
        mesh=fine,
        in_specs=placed,
        out_specs=(P(seq, head, None), P(seq + head, None)),
        check_vma=False,
    )
```

```python
import functools

import jax
import jax.numpy as jnp
import numpy as np
from jax import lax
from jax.experimental import pallas as pl
from jax.experimental.pallas import tpu as pltpu
from jax.sharding import Mesh
from jax.sharding import PartitionSpec as P

H_LOC = 4
DL = 512
DR = 64
DK = 576
TILE = 256
HALF = 128
NG = 8
KEYS = NG * TILE
LOG2E = 1.4426950408889634
FLOOR = -1e30
LANES = 128
OWNED = 32
PACKED = OWNED * DK // LANES
MAIN_VMEM = 20 * 1024 * 1024
FIRST = 5
WHOLE = 5
SWAPPED = (3, 4)

softmax_scale = 0.07216878364870322

BF = jnp.bfloat16
F32 = jnp.float32


def dot(a, b):
    return lax.dot_general(a, b, (((1,), (0,)), ((), ())), preferred_element_type=F32)


def dot_nt(a, b):
    return lax.dot_general(a, b, (((1,), (1,)), ((), ())), preferred_element_type=F32)


def directions(place_ref):
    core, zl = place_ref[0], place_ref[2]
    turn = 2 * core
    ahead = [(0 - dy) & 3 for dy in (0, 1 + turn, 1 + turn, 3 - turn, 3 - turn, 0, 2, 2)]
    floors = [zl ^ dz for dz in (0, 0, 1, 0, 1, 1, 0, 1)]
    return ahead, floors


def positions(place_ref, query_blocks_ref, key_blocks_ref):
    core, y, zl = (place_ref[n] for n in range(3))
    ahead, floors = directions(place_ref)
    mine = query_blocks_ref[y * 2 + zl]
    limits = []
    for up, floor in zip(ahead, floors):
        lag = (mine - key_blocks_ref[((y + up) & 3) * 2 + floor]) * TILE
        limits.append((lag - core * 8, lag - (core ^ 1) * 8))
    return limits


def halves(refs):
    out = []
    for slot in range(min(WHOLE, len(refs))):
        flip = slot in SWAPPED
        blocks = [refs[slot][n * DK : (n + 1) * DK, :] for n in range(2)]
        out.append(blocks[::-1] if flip else blocks)
    rest = refs[WHOLE:]
    for slot in range(len(rest) // 2):
        out.append([rest[slot][...], rest[slot + len(rest) // 2][...]])
    return out


def offsets():
    t = lax.broadcasted_iota(jnp.int32, (HALF, TILE), 0)
    i = lax.broadcasted_iota(jnp.int32, (HALF, TILE), 1)
    return (t >> 3) * 16 + (t & 7) - i


def span(c):
    return slice(c * TILE, (c + 1) * TILE)


def weigh(keys, qt, got, delta, limits):
    scores = dot(keys, qt) * (softmax_scale * LOG2E)
    parts = [
        jnp.where(delta <= limits[b], scores[b * HALF : (b + 1) * HALF], -jnp.inf)
        for b in range(2)
    ]
    peak = jnp.maximum(*[jnp.max(p, axis=0, keepdims=True) for p in parts])
    floor = jnp.maximum(peak, FLOOR)
    e = [jnp.exp2(p - floor) for p in parts]
    total = sum(jnp.sum(p, axis=0, keepdims=True) for p in e)
    return e, dot(keys[:, :DL], got), peak, total


def first_kernel(place_ref, query_blocks_ref, key_blocks_ref, qt_ref, go_ref, *refs):
    e_ref, gp_ref, stat_ref, gl_ref, gr_ref, got_ref, k_s = refs[FIRST:]
    limits = positions(place_ref, query_blocks_ref, key_blocks_ref)
    for slot, pair in enumerate(halves(refs[:FIRST])):
        for b in range(2):
            at = slot * TILE + b * HALF
            k_s[at : at + HALF, :] = pair[b].T
    delta = offsets()
    for h in range(H_LOC):
        go = go_ref[h]
        gl_ref[h * 2 * TILE : h * 2 * TILE + TILE, :] = go
        got_ref[h] = go.T
        q = qt_ref[h].T
        gl_ref[h * 2 * TILE + TILE : (h + 1) * 2 * TILE, :] = q[:, :DL]
        gr_ref[h * TILE : (h + 1) * TILE, :] = q[:, DL:]
        for c in range(FIRST):
            e, gp, peak, total = weigh(k_s[span(c), :], qt_ref[h], got_ref[h], delta, limits[c])
            for b in range(2):
                at = c * TILE + b * HALF
                e_ref[h, at : at + HALF, :] = e[b]
            gp_ref[h, span(c), :] = gp
            stat_ref[0, h, c : c + 1, :] = peak
            stat_ref[1, h, c : c + 1, :] = total


def to_keys(place_ref, half, w_ref, gl_ref, gr_ref, ref):
    ahead, floors = directions(place_ref)
    core, x = place_ref[0], place_ref[3]
    later = core ^ half
    for c in range(NG // 2):
        w = w_ref[span(c), :]
        lat = dot(w, gl_ref[...])
        wr = jnp.concatenate(
            [w[:, (2 * h + 1) * TILE : (2 * h + 2) * TILE] for h in range(H_LOC)], axis=1
        )
        rope = dot(wr, gr_ref[...])
        for b in range(2):
            slot = 2 * c + b
            for to in range(4):
                at = b * HALF + to * OWNED
                right = (to - x) & 3
                i = jnp.where(later == 0, right, ahead[slot])
                j = jnp.where(later == 0, ahead[slot], right)
                for n in range(DL // LANES):
                    ref[i, j, floors[slot], n * OWNED : (n + 1) * OWNED, :] = lat[
                        at : at + OWNED, n * LANES : (n + 1) * LANES
                    ].astype(ref.dtype)
                both = jnp.concatenate(
                    [rope[at : at + OWNED // 2], rope[at + OWNED // 2 : at + OWNED]], axis=1
                )
                ref[i, j, floors[slot], DL // LANES * OWNED :, :] = both.astype(ref.dtype)


def main_kernel(place_ref, query_blocks_ref, key_blocks_ref, qt_ref, *refs):
    k_refs, refs = refs[: 2 * NG - WHOLE], refs[2 * NG - WHOLE :]
    e1_ref, gp1_ref, stat_ref, gl_ref, gr_ref, got_ref = refs[:6]
    dqt_ref, own_w_ref, other_ref, kt_s, k_s, e_s, gp_s, other_w_s = refs[6:]
    limits = positions(place_ref, query_blocks_ref, key_blocks_ref)
    w_refs = (own_w_ref, other_w_s)
    for slot, pair in enumerate(halves(k_refs)):
        for b in range(2):
            at = b * KEYS // 2 + slot * HALF
            kt_s[:, at : at + HALF] = pair[b]
            if slot >= FIRST:
                at = (slot - FIRST) * TILE + b * HALF
                k_s[at : at + HALF, :] = pair[b].T
    delta = offsets()
    peaks = [[stat_ref[0, h, c : c + 1, :] for c in range(FIRST)] for h in range(H_LOC)]
    sums = [[stat_ref[1, h, c : c + 1, :] for c in range(FIRST)] for h in range(H_LOC)]
    factors = [None] * H_LOC
    corrs = [None] * H_LOC

    def load(h, c):
        if c < FIRST:
            return e1_ref[h, span(c), :], gp1_ref[h, span(c), :]
        return e_s[h, span(c - FIRST), :], gp_s[h, span(c - FIRST), :]

    def keep(h, c, kind, value):
        at = (2 * h + kind) * TILE
        for b, ref in enumerate(w_refs):
            ref[c * HALF : (c + 1) * HALF, at : at + TILE] = value[b * HALF : (b + 1) * HALF]

    def settle(h):
        peak = functools.reduce(jnp.maximum, peaks[h])
        shares = [jnp.exp2(p - peak) for p in peaks[h]]
        inv = 1.0 / sum(f * s for f, s in zip(shares, sums[h]))
        factors[h] = [f * inv for f in shares]
        corrs[h] = jnp.zeros((1, TILE), F32)

    def correct(h, c):
        e, gp = load(h, c)
        pb = (e * factors[h][c]).astype(BF)
        keep(h, c, 0, pb)
        corrs[h] = corrs[h] + jnp.sum(pb.astype(F32) * gp, axis=0, keepdims=True)

    def differ(h, c):
        e, gp = load(h, c)
        ds = (e * (factors[h][c] * softmax_scale) * (gp - corrs[h])).astype(BF)
        keep(h, c, 1, ds)

    def to_queries(h):
        for r in range(2):
            rows = slice(r * DK // 2, (r + 1) * DK // 2)
            at = (2 * h + 1) * TILE
            out = dot(kt_s[rows, : KEYS // 2], own_w_ref[:, at : at + TILE])
            out = out + dot(kt_s[rows, KEYS // 2 :], other_w_s[:, at : at + TILE])
            dqt_ref[h, rows, :] = out.astype(BF)

    for step in range(H_LOC + 2):
        if 1 <= step <= H_LOC:
            settle(step - 1)
        for c in range(NG):
            if step < H_LOC and c >= FIRST:
                e, gp, peak, total = weigh(
                    k_s[span(c - FIRST), :], qt_ref[step], got_ref[step], delta, limits[c]
                )
                for b in range(2):
                    at = (c - FIRST) * TILE + b * HALF
                    e_s[step, at : at + HALF, :] = e[b]
                gp_s[step, span(c - FIRST), :] = gp
                peaks[step].append(peak)
                sums[step].append(total)
            if 1 <= step <= H_LOC:
                correct(step - 1, c)
            if step >= 2:
                differ(step - 2, c)
        if step >= 2:
            to_queries(step - 2)
    to_keys(place_ref, 1, other_w_s, gl_ref, gr_ref, other_ref)


def own_kernel(place_ref, w_ref, gl_ref, gr_ref, own_ref):
    to_keys(place_ref, 0, w_ref, gl_ref, gr_ref, own_ref)


VMEM = pl.BlockSpec(memory_space=pltpu.VMEM)
SMEM = pl.BlockSpec(memory_space=pltpu.SMEM)


def first_part(place, query_blocks, key_blocks, qt, go, k_blocks):
    shapes = [
        ((H_LOC, FIRST * TILE, TILE), F32),
        ((H_LOC, FIRST * TILE, TILE), F32),
        ((2, H_LOC, 8, TILE), F32),
        ((H_LOC * 2 * TILE, DL), BF),
        ((H_LOC * TILE, DR), BF),
        ((H_LOC, DL, TILE), BF),
    ]
    return pl.pallas_call(
        first_kernel,
        in_specs=[SMEM] * 3 + [VMEM] * (2 + FIRST),
        out_specs=[VMEM] * len(shapes),
        out_shape=[jax.ShapeDtypeStruct(*s) for s in shapes],
        scratch_shapes=[pltpu.VMEM((FIRST * TILE, DK), BF)],
        cost_estimate=pl.CostEstimate(
            flops=2 * 1024 * FIRST * TILE * (DK + DL), bytes_accessed=20_000_000, transcendentals=0
        ),
        compiler_params=pltpu.CompilerParams(vmem_limit_bytes=20 * 1024 * 1024),
    )(place, query_blocks, key_blocks, qt, go, *k_blocks)


def main_part(place, query_blocks, key_blocks, qt, k_blocks, early):
    rest = (NG - FIRST) * TILE
    return pl.pallas_call(
        main_kernel,
        in_specs=[SMEM] * 3 + [VMEM] * (1 + len(k_blocks) + len(early)),
        out_specs=[VMEM] * 3,
        out_shape=[
            jax.ShapeDtypeStruct((H_LOC, DK, TILE), BF),
            jax.ShapeDtypeStruct((KEYS // 2, H_LOC * 2 * TILE), BF),
            jax.ShapeDtypeStruct((4, 4, 2, PACKED, LANES), BF),
        ],
        scratch_shapes=[
            pltpu.VMEM((DK, KEYS), BF),
            pltpu.VMEM((rest, DK), BF),
            pltpu.VMEM((H_LOC, rest, TILE), F32),
            pltpu.VMEM((H_LOC, rest, TILE), F32),
            pltpu.VMEM((KEYS // 2, H_LOC * 2 * TILE), BF),
        ],
        compiler_params=pltpu.CompilerParams(vmem_limit_bytes=MAIN_VMEM),
    )(place, query_blocks, key_blocks, qt, *k_blocks, *early)


def own_part(place, weights, gl, gr):
    return pl.pallas_call(
        own_kernel,
        in_specs=[SMEM] + [VMEM] * 3,
        out_specs=VMEM,
        out_shape=jax.ShapeDtypeStruct((4, 4, 2, PACKED, LANES), F32),
        cost_estimate=pl.CostEstimate(
            flops=KEYS * H_LOC * 2 * TILE * DK, bytes_accessed=9_000_000, transcendentals=0
        ),
        compiler_params=pltpu.CompilerParams(vmem_limit_bytes=12 * 1024 * 1024),
    )(place, weights, gl, gr)


def swap_cores(x):
    return lax.ppermute(x, "c", [(0, 1), (1, 0)])


def onward(x, dz):
    pairs = [
        ((y * 2 + z) * 2 + c, ((y + 1 - 2 * c) % 4 * 2 + (z ^ dz)) * 2 + c)
        for y in range(4)
        for z in range(2)
        for c in range(2)
    ]
    return lax.ppermute(x, ("y", "zl", "c"), pairs)


def crossed(x, first, step):
    def target(n):
        y, x, c = n // 8, n // 2 % 4, n % 2
        if (c == 0) == first:
            x = (x + step) % 4
        else:
            y = (y + step) % 4
        return (y * 4 + x) * 2 + c

    return lax.ppermute(x, ("y", "x", "c"), [(n, target(n)) for n in range(32)])


def unpack(x):
    lat = x[: DL // LANES * OWNED].reshape(DL // LANES, 4, 8, LANES)
    lat = lat.transpose(1, 2, 0, 3).reshape(4, 8, DL)
    rope = x[DL // LANES * OWNED :].reshape(2, 8, 2, DR).transpose(2, 0, 1, 3).reshape(4, 8, DR)
    return jnp.concatenate([lat, rope], axis=2)


def shards(queries, latent_cache, grad_output, query_blocks, key_blocks):
    core, y, zl, x = (lax.axis_index(a) for a in ("c", "y", "zl", "x"))
    row = lax.broadcasted_iota(jnp.int32, (TILE, TILE), 0)
    t = lax.broadcasted_iota(jnp.int32, (TILE, TILE), 1)
    half, t = t >> 7, t & 127
    pick = (row == (t >> 3) * 16 + (core ^ half) * 8 + (t & 7)).astype(BF)
    here = lax.dot_general(
        latent_cache, pick, (((0,), (0,)), ((), ())), preferred_element_type=F32
    ).astype(BF)
    here = jnp.concatenate([here[:, :HALF], here[:, HALF:]], axis=0)

    near = onward(here, 0)
    slant = onward(here, 1)
    beside = lax.ppermute(here[:DK], "zl", [(0, 1), (1, 0)])

    place = jnp.stack([core, y, zl, x])
    qt = queries.transpose(1, 2, 0)
    go = grad_output.transpose(1, 0, 2)
    go, beside, near, slant = lax.optimization_barrier((go, beside, near, slant))
    singles = [beside, onward(near[:DK], 0), onward(slant[:DK], 0)]
    swapped = [swap_cores(near), swap_cores(slant)]
    early = list(first_part(place, query_blocks, key_blocks, qt, go, [here, near, slant] + swapped))
    early[2], *singles = lax.optimization_barrier((early[2], *singles))
    blocks = [here, near, slant] + swapped + singles + [swap_cores(k) for k in singles]
    dqt, weights, other = main_part(place, query_blocks, key_blocks, qt, blocks, early)
    other = swap_cores(other)
    own = own_part(place, weights, early[3], early[4])

    sums = [own[d] + other[d].astype(F32) for d in range(4)]
    for first in (True, False):
        got = [crossed(sums[d].astype(BF), first, d) for d in (2, 1, 3)]
        sums = sums[0] + sum(g.astype(F32) for g in got)
    part = jnp.concatenate([unpack(sums[z]).astype(BF) for z in range(2)], axis=0)
    got = lax.all_to_all(part, ("zl", "zh"), 0, 0, tiled=True)
    return dqt.transpose(2, 0, 1), jnp.sum(got.astype(F32), axis=0)


def solution(mesh):
    fine = Mesh(mesh.devices.reshape(4, 2, 4, 4, 2), ("y", "zl", "x", "zh", "c"))
    seq, head = ("y", "zl"), ("x", "zh", "c")
    placed = (P(seq, head, None), P(seq, None), P(seq, head, None), P(), P())
    return jax.shard_map(
        shards,
        mesh=fine,
        in_specs=placed,
        out_specs=(P(seq, head, None), P(seq + head, None)),
        check_vma=False,
    )
```

```python
import functools

import jax
import jax.numpy as jnp
import numpy as np
from jax import lax
from jax.experimental import pallas as pl
from jax.experimental.pallas import tpu as pltpu
from jax.sharding import Mesh
from jax.sharding import PartitionSpec as P

H_LOC = 4
DL = 512
DR = 64
DK = 576
TILE = 256
HALF = 128
NG = 8
KEYS = NG * TILE
LOG2E = 1.4426950408889634
FLOOR = -1e30
LANES = 128
OWNED = 32
PACKED = OWNED * DK // LANES
MAIN_VMEM = 23 * 1024 * 1024
FIRST = 3

softmax_scale = 0.07216878364870322

BF = jnp.bfloat16
F32 = jnp.float32


def dot(a, b):
    return lax.dot_general(a, b, (((1,), (0,)), ((), ())), preferred_element_type=F32)


def dot_nt(a, b):
    return lax.dot_general(a, b, (((1,), (1,)), ((), ())), preferred_element_type=F32)


def directions(place_ref):
    core, zl = place_ref[0], place_ref[2]
    turn = 2 * core
    ahead = [(0 - dy) & 3 for dy in (0, 1 + turn, 1 + turn, 3 - turn, 3 - turn, 0, 2, 2)]
    floors = [zl ^ dz for dz in (0, 0, 1, 0, 1, 1, 0, 1)]
    return ahead, floors


def positions(place_ref, query_blocks_ref, key_blocks_ref):
    core, y, zl = (place_ref[n] for n in range(3))
    ahead, floors = directions(place_ref)
    mine = query_blocks_ref[y * 2 + zl]
    limits = []
    for up, floor in zip(ahead, floors):
        lag = (mine - key_blocks_ref[((y + up) & 3) * 2 + floor]) * TILE
        limits.append((lag - core * 8, lag - (core ^ 1) * 8))
    return limits


def halves(refs):
    return [[ref[...] for ref in refs[2 * n : 2 * n + 2]] for n in range(len(refs) // 2)]


def offsets():
    t = lax.broadcasted_iota(jnp.int32, (HALF, TILE), 0)
    i = lax.broadcasted_iota(jnp.int32, (HALF, TILE), 1)
    return (t >> 3) * 16 + (t & 7) - i


def span(c):
    return slice(c * TILE, (c + 1) * TILE)


def weigh(keys, qt, got, delta, limits):
    scores = dot(keys, qt) * (softmax_scale * LOG2E)
    parts = [
        jnp.where(delta <= limits[b], scores[b * HALF : (b + 1) * HALF], -jnp.inf)
        for b in range(2)
    ]
    peak = jnp.maximum(*[jnp.max(p, axis=0, keepdims=True) for p in parts])
    floor = jnp.maximum(peak, FLOOR)
    e = [jnp.exp2(p - floor) for p in parts]
    total = sum(jnp.sum(p, axis=0, keepdims=True) for p in e)
    return e, dot(keys[:, :DL], got), peak, total


def first_kernel(place_ref, query_blocks_ref, key_blocks_ref, qt_ref, go_ref, *refs):
    e_ref, gp_ref, stat_ref, gl_ref, gr_ref, got_ref, k_s = refs[2 * FIRST :]
    limits = positions(place_ref, query_blocks_ref, key_blocks_ref)
    for slot, pair in enumerate(halves(refs[: 2 * FIRST])):
        for b in range(2):
            at = slot * TILE + b * HALF
            k_s[at : at + HALF, :] = pair[b].T
    delta = offsets()
    for h in range(H_LOC):
        go = go_ref[h]
        gl_ref[h * 2 * TILE : h * 2 * TILE + TILE, :] = go
        got_ref[h] = go.T
        q = qt_ref[h].T
        gl_ref[h * 2 * TILE + TILE : (h + 1) * 2 * TILE, :] = q[:, :DL]
        gr_ref[h * TILE : (h + 1) * TILE, :] = q[:, DL:]
        for c in range(FIRST):
            e, gp, peak, total = weigh(k_s[span(c), :], qt_ref[h], got_ref[h], delta, limits[c])
            for b in range(2):
                at = c * TILE + b * HALF
                e_ref[h, at : at + HALF, :] = e[b]
            gp_ref[h, span(c), :] = gp
            stat_ref[0, h, c : c + 1, :] = peak
            stat_ref[1, h, c : c + 1, :] = total


def to_keys(place_ref, half, w_ref, gl_ref, gr_ref, ref):
    ahead, floors = directions(place_ref)
    core, x = place_ref[0], place_ref[3]
    later = core ^ half
    for c in range(NG // 2):
        w = w_ref[span(c), :]
        lat = dot(w, gl_ref[...])
        wr = jnp.concatenate(
            [w[:, (2 * h + 1) * TILE : (2 * h + 2) * TILE] for h in range(H_LOC)], axis=1
        )
        rope = dot(wr, gr_ref[...])
        for b in range(2):
            slot = 2 * c + b
            for to in range(4):
                at = b * HALF + to * OWNED
                right = (to - x) & 3
                i = jnp.where(later == 0, right, ahead[slot])
                j = jnp.where(later == 0, ahead[slot], right)
                for n in range(DL // LANES):
                    ref[i, j, floors[slot], n * OWNED : (n + 1) * OWNED, :] = lat[
                        at : at + OWNED, n * LANES : (n + 1) * LANES
                    ].astype(ref.dtype)
                both = jnp.concatenate(
                    [rope[at : at + OWNED // 2], rope[at + OWNED // 2 : at + OWNED]], axis=1
                )
                ref[i, j, floors[slot], DL // LANES * OWNED :, :] = both.astype(ref.dtype)


def main_kernel(place_ref, query_blocks_ref, key_blocks_ref, qt_ref, *refs):
    k_refs, refs = refs[: 2 * NG], refs[2 * NG :]
    e1_ref, gp1_ref, stat_ref, gl_ref, gr_ref, got_ref = refs[:6]
    dqt_ref, own_w_ref, other_ref, kt_s, k_s, e_s, gp_s, other_w_s = refs[6:]
    limits = positions(place_ref, query_blocks_ref, key_blocks_ref)
    w_refs = (own_w_ref, other_w_s)
    for slot, pair in enumerate(halves(k_refs)):
        for b in range(2):
            at = b * KEYS // 2 + slot * HALF
            kt_s[:, at : at + HALF] = pair[b]
            if slot >= FIRST:
                at = (slot - FIRST) * TILE + b * HALF
                k_s[at : at + HALF, :] = pair[b].T
    delta = offsets()
    peaks = [[stat_ref[0, h, c : c + 1, :] for c in range(FIRST)] for h in range(H_LOC)]
    sums = [[stat_ref[1, h, c : c + 1, :] for c in range(FIRST)] for h in range(H_LOC)]
    factors = [None] * H_LOC
    corrs = [None] * H_LOC

    def load(h, c):
        if c < FIRST:
            return e1_ref[h, span(c), :], gp1_ref[h, span(c), :]
        return e_s[h, span(c - FIRST), :], gp_s[h, span(c - FIRST), :]

    def keep(h, c, kind, value):
        at = (2 * h + kind) * TILE
        for b, ref in enumerate(w_refs):
            ref[c * HALF : (c + 1) * HALF, at : at + TILE] = value[b * HALF : (b + 1) * HALF]

    def settle(h):
        peak = functools.reduce(jnp.maximum, peaks[h])
        shares = [jnp.exp2(p - peak) for p in peaks[h]]
        inv = 1.0 / sum(f * s for f, s in zip(shares, sums[h]))
        factors[h] = [f * inv for f in shares]
        corrs[h] = jnp.zeros((1, TILE), F32)

    def correct(h, c):
        e, gp = load(h, c)
        pb = (e * factors[h][c]).astype(BF)
        keep(h, c, 0, pb)
        corrs[h] = corrs[h] + jnp.sum(pb.astype(F32) * gp, axis=0, keepdims=True)

    def differ(h, c):
        e, gp = load(h, c)
        ds = (e * (factors[h][c] * softmax_scale) * (gp - corrs[h])).astype(BF)
        keep(h, c, 1, ds)

    def to_queries(h):
        for r in range(2):
            rows = slice(r * DK // 2, (r + 1) * DK // 2)
            at = (2 * h + 1) * TILE
            out = dot(kt_s[rows, : KEYS // 2], own_w_ref[:, at : at + TILE])
            out = out + dot(kt_s[rows, KEYS // 2 :], other_w_s[:, at : at + TILE])
            dqt_ref[h, rows, :] = out.astype(BF)

    for step in range(H_LOC + 2):
        if 1 <= step <= H_LOC:
            settle(step - 1)
        for c in range(NG):
            if step < H_LOC and c >= FIRST:
                e, gp, peak, total = weigh(
                    k_s[span(c - FIRST), :], qt_ref[step], got_ref[step], delta, limits[c]
                )
                for b in range(2):
                    at = (c - FIRST) * TILE + b * HALF
                    e_s[step, at : at + HALF, :] = e[b]
                gp_s[step, span(c - FIRST), :] = gp
                peaks[step].append(peak)
                sums[step].append(total)
            if 1 <= step <= H_LOC:
                correct(step - 1, c)
            if step >= 2:
                differ(step - 2, c)
        if step >= 2:
            to_queries(step - 2)
    to_keys(place_ref, 1, other_w_s, gl_ref, gr_ref, other_ref)


def own_kernel(place_ref, w_ref, gl_ref, gr_ref, own_ref):
    to_keys(place_ref, 0, w_ref, gl_ref, gr_ref, own_ref)


VMEM = pl.BlockSpec(memory_space=pltpu.VMEM)
SMEM = pl.BlockSpec(memory_space=pltpu.SMEM)


def first_part(place, query_blocks, key_blocks, qt, go, k_blocks):
    shapes = [
        ((H_LOC, FIRST * TILE, TILE), F32),
        ((H_LOC, FIRST * TILE, TILE), F32),
        ((2, H_LOC, 8, TILE), F32),
        ((H_LOC * 2 * TILE, DL), BF),
        ((H_LOC * TILE, DR), BF),
        ((H_LOC, DL, TILE), BF),
    ]
    return pl.pallas_call(
        first_kernel,
        in_specs=[SMEM] * 3 + [VMEM] * (2 + 2 * FIRST),
        out_specs=[VMEM] * len(shapes),
        out_shape=[jax.ShapeDtypeStruct(*s) for s in shapes],
        scratch_shapes=[pltpu.VMEM((FIRST * TILE, DK), BF)],
        cost_estimate=pl.CostEstimate(
            flops=2 * 1024 * FIRST * TILE * (DK + DL), bytes_accessed=20_000_000, transcendentals=0
        ),
        compiler_params=pltpu.CompilerParams(vmem_limit_bytes=16 * 1024 * 1024),
    )(place, query_blocks, key_blocks, qt, go, *k_blocks)


def main_part(place, query_blocks, key_blocks, qt, k_blocks, early):
    rest = (NG - FIRST) * TILE
    return pl.pallas_call(
        main_kernel,
        in_specs=[SMEM] * 3 + [VMEM] * (1 + len(k_blocks) + len(early)),
        out_specs=[VMEM] * 3,
        out_shape=[
            jax.ShapeDtypeStruct((H_LOC, DK, TILE), BF),
            jax.ShapeDtypeStruct((KEYS // 2, H_LOC * 2 * TILE), BF),
            jax.ShapeDtypeStruct((4, 4, 2, PACKED, LANES), BF),
        ],
        scratch_shapes=[
            pltpu.VMEM((DK, KEYS), BF),
            pltpu.VMEM((rest, DK), BF),
            pltpu.VMEM((H_LOC, rest, TILE), F32),
            pltpu.VMEM((H_LOC, rest, TILE), F32),
            pltpu.VMEM((KEYS // 2, H_LOC * 2 * TILE), BF),
        ],
        compiler_params=pltpu.CompilerParams(vmem_limit_bytes=MAIN_VMEM),
    )(place, query_blocks, key_blocks, qt, *k_blocks, *early)


def own_part(place, weights, gl, gr):
    return pl.pallas_call(
        own_kernel,
        in_specs=[SMEM] + [VMEM] * 3,
        out_specs=VMEM,
        out_shape=jax.ShapeDtypeStruct((4, 4, 2, PACKED, LANES), F32),
        cost_estimate=pl.CostEstimate(
            flops=KEYS * H_LOC * 2 * TILE * DK, bytes_accessed=9_000_000, transcendentals=0
        ),
        compiler_params=pltpu.CompilerParams(vmem_limit_bytes=12 * 1024 * 1024),
    )(place, weights, gl, gr)


def swap_cores(x):
    return lax.ppermute(x, "c", [(0, 1), (1, 0)])


def onward(x, dz):
    pairs = [
        ((y * 2 + z) * 2 + c, ((y + 1 - 2 * c) % 4 * 2 + (z ^ dz)) * 2 + c)
        for y in range(4)
        for z in range(2)
        for c in range(2)
    ]
    return lax.ppermute(x, ("y", "zl", "c"), pairs)


def crossed(x, first, step):
    def target(n):
        y, x, c = n // 8, n // 2 % 4, n % 2
        if (c == 0) == first:
            x = (x + step) % 4
        else:
            y = (y + step) % 4
        return (y * 4 + x) * 2 + c

    return lax.ppermute(x, ("y", "x", "c"), [(n, target(n)) for n in range(32)])


def unpack(x):
    lat = x[: DL // LANES * OWNED].reshape(DL // LANES, 4, 8, LANES)
    lat = lat.transpose(1, 2, 0, 3).reshape(4, 8, DL)
    rope = x[DL // LANES * OWNED :].reshape(2, 8, 2, DR).transpose(2, 0, 1, 3).reshape(4, 8, DR)
    return jnp.concatenate([lat, rope], axis=2)


def shards(queries, latent_cache, grad_output, query_blocks, key_blocks):
    core, y, zl, x = (lax.axis_index(a) for a in ("c", "y", "zl", "x"))
    row = lax.broadcasted_iota(jnp.int32, (TILE, TILE), 0)
    t = lax.broadcasted_iota(jnp.int32, (TILE, TILE), 1)
    half, t = t >> 7, t & 127
    pick = (row == (t >> 3) * 16 + (core ^ half) * 8 + (t & 7)).astype(BF)
    here = lax.dot_general(
        latent_cache, pick, (((0,), (0,)), ((), ())), preferred_element_type=F32
    ).astype(BF)
    mine, rest = here[:, :HALF], here[:, HALF:]

    slant = [onward(mine, 1)]
    near = [onward(mine, 0)]
    beside = lax.ppermute(mine, "zl", [(0, 1), (1, 0)])
    slant.append(onward(rest, 1))
    near.append(onward(rest, 0))
    place = jnp.stack([core, y, zl, x])

    qt = queries.transpose(1, 2, 0)
    go = grad_output.transpose(1, 0, 2)
    far = [onward(near[0], 0), onward(slant[0], 0)]
    blocks = [mine, rest] + near + slant
    early = list(first_part(place, query_blocks, key_blocks, qt, go, blocks))
    early[2], beside, *whole = lax.optimization_barrier((early[2], beside, *near, *slant))
    for pair in (whole[:2], whole[2:]):
        blocks += [swap_cores(pair[1]), swap_cores(pair[0])]
    early[2], *far = lax.optimization_barrier((early[2], *far))
    for k in [beside] + far:
        blocks += [k, swap_cores(k)]
    dqt, weights, other = main_part(place, query_blocks, key_blocks, qt, blocks, early)
    other = swap_cores(other)
    own = own_part(place, weights, early[3], early[4])

    sums = [own[d] + other[d].astype(F32) for d in range(4)]
    for first in (True, False):
        got = [crossed(sums[d].astype(BF), first, d) for d in (2, 1, 3)]
        sums = sums[0] + sum(g.astype(F32) for g in got)
    part = jnp.concatenate([unpack(sums[z]).astype(BF) for z in range(2)], axis=0)
    got = lax.all_to_all(part, ("zl", "zh"), 0, 0, tiled=True)
    return dqt.transpose(2, 0, 1), jnp.sum(got.astype(F32), axis=0)


def solution(mesh):
    fine = Mesh(mesh.devices.reshape(4, 2, 4, 4, 2), ("y", "zl", "x", "zh", "c"))
    seq, head = ("y", "zl"), ("x", "zh", "c")
    placed = (P(seq, head, None), P(seq, None), P(seq, head, None), P(), P())
    return jax.shard_map(
        shards,
        mesh=fine,
        in_specs=placed,
        out_specs=(P(seq, head, None), P(seq + head, None)),
        check_vma=False,
    )
```

```python
import functools

import jax
import jax.numpy as jnp
import numpy as np
from jax import lax
from jax.experimental import pallas as pl
from jax.experimental.pallas import tpu as pltpu
from jax.sharding import Mesh
from jax.sharding import PartitionSpec as P

H_LOC = 4
DL = 512
DR = 64
DK = 576
TILE = 256
HALF = 128
NG = 8
KEYS = NG * TILE
LOG2E = 1.4426950408889634
FLOOR = -1e30
LANES = 128
OWNED = 32
PACKED = OWNED * DK // LANES
MAIN_VMEM = 23 * 1024 * 1024
FIRST = 3

softmax_scale = 0.07216878364870322

BF = jnp.bfloat16
F32 = jnp.float32


def dot(a, b):
    return lax.dot_general(a, b, (((1,), (0,)), ((), ())), preferred_element_type=F32)


def dot_nt(a, b):
    return lax.dot_general(a, b, (((1,), (1,)), ((), ())), preferred_element_type=F32)


def directions(place_ref):
    core, zl = place_ref[0], place_ref[2]
    turn = 2 * core
    ahead = [(0 - dy) & 3 for dy in (0, 1 + turn, 1 + turn, 3 - turn, 3 - turn, 0, 2, 2)]
    floors = [zl ^ dz for dz in (0, 0, 1, 0, 1, 1, 0, 1)]
    return ahead, floors


def positions(place_ref, query_blocks_ref, key_blocks_ref):
    core, y, zl = (place_ref[n] for n in range(3))
    ahead, floors = directions(place_ref)
    mine = query_blocks_ref[y * 2 + zl]
    limits = []
    for up, floor in zip(ahead, floors):
        lag = (mine - key_blocks_ref[((y + up) & 3) * 2 + floor]) * TILE
        limits.append((lag - core * 8, lag - (core ^ 1) * 8))
    return limits


def halves(refs):
    return [[ref[...] for ref in refs[2 * n : 2 * n + 2]] for n in range(len(refs) // 2)]


def offsets():
    t = lax.broadcasted_iota(jnp.int32, (HALF, TILE), 0)
    i = lax.broadcasted_iota(jnp.int32, (HALF, TILE), 1)
    return (t >> 3) * 16 + (t & 7) - i


def span(c):
    return slice(c * TILE, (c + 1) * TILE)


def weigh(keys, qt, got, delta, limits):
    scores = dot(keys, qt) * (softmax_scale * LOG2E)
    parts = [
        jnp.where(delta <= limits[b], scores[b * HALF : (b + 1) * HALF], -jnp.inf)
        for b in range(2)
    ]
    peak = jnp.maximum(*[jnp.max(p, axis=0, keepdims=True) for p in parts])
    floor = jnp.maximum(peak, FLOOR)
    e = [jnp.exp2(p - floor) for p in parts]
    total = sum(jnp.sum(p, axis=0, keepdims=True) for p in e)
    return e, dot(keys[:, :DL], got), peak, total


def first_kernel(place_ref, query_blocks_ref, key_blocks_ref, qt_ref, go_ref, *refs):
    e_ref, gp_ref, stat_ref, gl_ref, gr_ref, got_ref, k_s = refs[2 * FIRST :]
    limits = positions(place_ref, query_blocks_ref, key_blocks_ref)
    for slot, pair in enumerate(halves(refs[: 2 * FIRST])):
        for b in range(2):
            at = slot * TILE + b * HALF
            k_s[at : at + HALF, :] = pair[b].T
    delta = offsets()
    for h in range(H_LOC):
        go = go_ref[h]
        gl_ref[h * 2 * TILE : h * 2 * TILE + TILE, :] = go
        got_ref[h] = go.T
        q = qt_ref[h].T
        gl_ref[h * 2 * TILE + TILE : (h + 1) * 2 * TILE, :] = q[:, :DL]
        gr_ref[h * TILE : (h + 1) * TILE, :] = q[:, DL:]
        for c in range(FIRST):
            e, gp, peak, total = weigh(k_s[span(c), :], qt_ref[h], got_ref[h], delta, limits[c])
            for b in range(2):
                at = c * TILE + b * HALF
                e_ref[h, at : at + HALF, :] = e[b]
            gp_ref[h, span(c), :] = gp
            stat_ref[0, h, c : c + 1, :] = peak
            stat_ref[1, h, c : c + 1, :] = total


def to_keys(place_ref, half, w_ref, gl_ref, gr_ref, ref):
    ahead, floors = directions(place_ref)
    core, x = place_ref[0], place_ref[3]
    later = core ^ half
    for c in range(NG // 2):
        w = w_ref[span(c), :]
        lat = dot(w, gl_ref[...])
        wr = jnp.concatenate(
            [w[:, (2 * h + 1) * TILE : (2 * h + 2) * TILE] for h in range(H_LOC)], axis=1
        )
        rope = dot(wr, gr_ref[...])
        for b in range(2):
            slot = 2 * c + b
            for to in range(4):
                at = b * HALF + to * OWNED
                right = (to - x) & 3
                i = jnp.where(later == 0, right, ahead[slot])
                j = jnp.where(later == 0, ahead[slot], right)
                for n in range(DL // LANES):
                    ref[i, j, floors[slot], n * OWNED : (n + 1) * OWNED, :] = lat[
                        at : at + OWNED, n * LANES : (n + 1) * LANES
                    ].astype(ref.dtype)
                both = jnp.concatenate(
                    [rope[at : at + OWNED // 2], rope[at + OWNED // 2 : at + OWNED]], axis=1
                )
                ref[i, j, floors[slot], DL // LANES * OWNED :, :] = both.astype(ref.dtype)


def main_kernel(place_ref, query_blocks_ref, key_blocks_ref, qt_ref, *refs):
    k_refs, refs = refs[: 2 * NG], refs[2 * NG :]
    e1_ref, gp1_ref, stat_ref, gl_ref, gr_ref, got_ref = refs[:6]
    own_w_ref, other_w_s, other_ref, kt_s, k_s, e_s, gp_s = refs[6:]
    limits = positions(place_ref, query_blocks_ref, key_blocks_ref)
    w_refs = (own_w_ref, other_w_s)
    for slot, pair in enumerate(halves(k_refs)):
        for b in range(2):
            at = b * KEYS // 2 + slot * HALF
            kt_s[:, at : at + HALF] = pair[b]
            if slot >= FIRST:
                at = (slot - FIRST) * TILE + b * HALF
                k_s[at : at + HALF, :] = pair[b].T
    delta = offsets()
    peaks = [[stat_ref[0, h, c : c + 1, :] for c in range(FIRST)] for h in range(H_LOC)]
    sums = [[stat_ref[1, h, c : c + 1, :] for c in range(FIRST)] for h in range(H_LOC)]
    factors = [None] * H_LOC
    corrs = [None] * H_LOC

    def load(h, c):
        if c < FIRST:
            return e1_ref[h, span(c), :], gp1_ref[h, span(c), :]
        return e_s[h, span(c - FIRST), :], gp_s[h, span(c - FIRST), :]

    def keep(h, c, kind, value):
        at = (2 * h + kind) * TILE
        for b, ref in enumerate(w_refs):
            ref[c * HALF : (c + 1) * HALF, at : at + TILE] = value[b * HALF : (b + 1) * HALF]

    def settle(h):
        peak = functools.reduce(jnp.maximum, peaks[h])
        shares = [jnp.exp2(p - peak) for p in peaks[h]]
        inv = 1.0 / sum(f * s for f, s in zip(shares, sums[h]))
        factors[h] = [f * inv for f in shares]
        corrs[h] = jnp.zeros((1, TILE), F32)

    def correct(h, c):
        e, gp = load(h, c)
        pb = (e * factors[h][c]).astype(BF)
        keep(h, c, 0, pb)
        corrs[h] = corrs[h] + jnp.sum(pb.astype(F32) * gp, axis=0, keepdims=True)

    def differ(h, c):
        e, gp = load(h, c)
        ds = (e * (factors[h][c] * softmax_scale) * (gp - corrs[h])).astype(BF)
        keep(h, c, 1, ds)

    for step in range(H_LOC + 2):
        if 1 <= step <= H_LOC:
            settle(step - 1)
        for c in range(NG):
            if step < H_LOC and c >= FIRST:
                e, gp, peak, total = weigh(
                    k_s[span(c - FIRST), :], qt_ref[step], got_ref[step], delta, limits[c]
                )
                for b in range(2):
                    at = (c - FIRST) * TILE + b * HALF
                    e_s[step, at : at + HALF, :] = e[b]
                gp_s[step, span(c - FIRST), :] = gp
                peaks[step].append(peak)
                sums[step].append(total)
            if 1 <= step <= H_LOC:
                correct(step - 1, c)
            if step >= 2:
                differ(step - 2, c)
    to_keys(place_ref, 1, other_w_s, gl_ref, gr_ref, other_ref)


def query_kernel(own_w_ref, other_w_ref, kt_ref, dqt_ref):
    for h in range(H_LOC):
        at = (2 * h + 1) * TILE
        for r in range(2):
            rows = slice(r * DK // 2, (r + 1) * DK // 2)
            out = dot(kt_ref[rows, : KEYS // 2], own_w_ref[:, at : at + TILE])
            out = out + dot(kt_ref[rows, KEYS // 2 :], other_w_ref[:, at : at + TILE])
            dqt_ref[h, rows, :] = out.astype(BF)


def own_kernel(place_ref, w_ref, gl_ref, gr_ref, own_ref):
    to_keys(place_ref, 0, w_ref, gl_ref, gr_ref, own_ref)


VMEM = pl.BlockSpec(memory_space=pltpu.VMEM)
SMEM = pl.BlockSpec(memory_space=pltpu.SMEM)


def first_part(place, query_blocks, key_blocks, qt, go, k_blocks):
    shapes = [
        ((H_LOC, FIRST * TILE, TILE), F32),
        ((H_LOC, FIRST * TILE, TILE), F32),
        ((2, H_LOC, 8, TILE), F32),
        ((H_LOC * 2 * TILE, DL), BF),
        ((H_LOC * TILE, DR), BF),
        ((H_LOC, DL, TILE), BF),
    ]
    return pl.pallas_call(
        first_kernel,
        in_specs=[SMEM] * 3 + [VMEM] * (2 + 2 * FIRST),
        out_specs=[VMEM] * len(shapes),
        out_shape=[jax.ShapeDtypeStruct(*s) for s in shapes],
        scratch_shapes=[pltpu.VMEM((FIRST * TILE, DK), BF)],
        cost_estimate=pl.CostEstimate(
            flops=2 * 1024 * FIRST * TILE * (DK + DL), bytes_accessed=20_000_000, transcendentals=0
        ),
        compiler_params=pltpu.CompilerParams(vmem_limit_bytes=16 * 1024 * 1024),
    )(place, query_blocks, key_blocks, qt, go, *k_blocks)


def main_part(place, query_blocks, key_blocks, qt, k_blocks, early):
    rest = (NG - FIRST) * TILE
    return pl.pallas_call(
        main_kernel,
        in_specs=[SMEM] * 3 + [VMEM] * (1 + len(k_blocks) + len(early)),
        out_specs=[VMEM] * 4,
        out_shape=[
            jax.ShapeDtypeStruct((KEYS // 2, H_LOC * 2 * TILE), BF),
            jax.ShapeDtypeStruct((KEYS // 2, H_LOC * 2 * TILE), BF),
            jax.ShapeDtypeStruct((4, 4, 2, PACKED, LANES), BF),
            jax.ShapeDtypeStruct((DK, KEYS), BF),
        ],
        scratch_shapes=[
            pltpu.VMEM((rest, DK), BF),
            pltpu.VMEM((H_LOC, rest, TILE), F32),
            pltpu.VMEM((H_LOC, rest, TILE), F32),
        ],
        compiler_params=pltpu.CompilerParams(vmem_limit_bytes=MAIN_VMEM),
    )(place, query_blocks, key_blocks, qt, *k_blocks, *early)


def query_part(own_weights, other_weights, kt):
    return pl.pallas_call(
        query_kernel,
        in_specs=[VMEM] * 3,
        out_specs=VMEM,
        out_shape=jax.ShapeDtypeStruct((H_LOC, DK, TILE), BF),
        cost_estimate=pl.CostEstimate(
            flops=2 * KEYS * H_LOC * TILE * DK, bytes_accessed=12_000_000, transcendentals=0
        ),
        compiler_params=pltpu.CompilerParams(vmem_limit_bytes=16 * 1024 * 1024),
    )(own_weights, other_weights, kt)


def own_part(place, weights, gl, gr):
    return pl.pallas_call(
        own_kernel,
        in_specs=[SMEM] + [VMEM] * 3,
        out_specs=VMEM,
        out_shape=jax.ShapeDtypeStruct((4, 4, 2, PACKED, LANES), F32),
        cost_estimate=pl.CostEstimate(
            flops=KEYS * H_LOC * 2 * TILE * DK, bytes_accessed=9_000_000, transcendentals=0
        ),
        compiler_params=pltpu.CompilerParams(vmem_limit_bytes=12 * 1024 * 1024),
    )(place, weights, gl, gr)


def swap_cores(x):
    return lax.ppermute(x, "c", [(0, 1), (1, 0)])


def onward(x, dz):
    pairs = [
        ((y * 2 + z) * 2 + c, ((y + 1 - 2 * c) % 4 * 2 + (z ^ dz)) * 2 + c)
        for y in range(4)
        for z in range(2)
        for c in range(2)
    ]
    return lax.ppermute(x, ("y", "zl", "c"), pairs)


def crossed(x, first, step):
    def target(n):
        y, x, c = n // 8, n // 2 % 4, n % 2
        if (c == 0) == first:
            x = (x + step) % 4
        else:
            y = (y + step) % 4
        return (y * 4 + x) * 2 + c

    return lax.ppermute(x, ("y", "x", "c"), [(n, target(n)) for n in range(32)])


def unpack(x):
    lat = x[: DL // LANES * OWNED].reshape(DL // LANES, 4, 8, LANES)
    lat = lat.transpose(1, 2, 0, 3).reshape(4, 8, DL)
    rope = x[DL // LANES * OWNED :].reshape(2, 8, 2, DR).transpose(2, 0, 1, 3).reshape(4, 8, DR)
    return jnp.concatenate([lat, rope], axis=2)


def shards(queries, latent_cache, grad_output, query_blocks, key_blocks):
    core, y, zl, x = (lax.axis_index(a) for a in ("c", "y", "zl", "x"))
    row = lax.broadcasted_iota(jnp.int32, (TILE, TILE), 0)
    t = lax.broadcasted_iota(jnp.int32, (TILE, TILE), 1)
    half, t = t >> 7, t & 127
    pick = (row == (t >> 3) * 16 + (core ^ half) * 8 + (t & 7)).astype(BF)
    here = lax.dot_general(
        latent_cache, pick, (((0,), (0,)), ((), ())), preferred_element_type=F32
    ).astype(BF)
    mine, rest = here[:, :HALF], here[:, HALF:]

    slant = [onward(mine, 1)]
    near = [onward(mine, 0)]
    beside = lax.ppermute(mine, "zl", [(0, 1), (1, 0)])
    slant.append(onward(rest, 1))
    near.append(onward(rest, 0))
    place = jnp.stack([core, y, zl, x])

    qt = queries.transpose(1, 2, 0)
    go = grad_output.transpose(1, 0, 2)
    far = [onward(near[0], 0), onward(slant[0], 0)]
    blocks = [mine, rest] + near + slant
    early = list(first_part(place, query_blocks, key_blocks, qt, go, blocks))
    early[2], beside, *whole = lax.optimization_barrier((early[2], beside, *near, *slant))
    for pair in (whole[:2], whole[2:]):
        blocks += [swap_cores(pair[1]), swap_cores(pair[0])]
    early[2], *far = lax.optimization_barrier((early[2], *far))
    for k in [beside] + far:
        blocks += [k, swap_cores(k)]
    weights, other_weights, other, kt = main_part(place, query_blocks, key_blocks, qt, blocks, early)
    dqt = query_part(weights, other_weights, kt)
    other = swap_cores(other)
    own = own_part(place, weights, early[3], early[4])

    sums = [own[d] + other[d].astype(F32) for d in range(4)]
    for first in (True, False):
        got = [crossed(sums[d].astype(BF), first, d) for d in (2, 1, 3)]
        sums = sums[0] + sum(g.astype(F32) for g in got)
    part = jnp.concatenate([unpack(sums[z]).astype(BF) for z in range(2)], axis=0)
    got = lax.all_to_all(part, ("zl", "zh"), 0, 0, tiled=True)
    return dqt.transpose(2, 0, 1), jnp.sum(got.astype(F32), axis=0)


def solution(mesh):
    fine = Mesh(mesh.devices.reshape(4, 2, 4, 4, 2), ("y", "zl", "x", "zh", "c"))
    seq, head = ("y", "zl"), ("x", "zh", "c")
    placed = (P(seq, head, None), P(seq, None), P(seq, head, None), P(), P())
    return jax.shard_map(
        shards,
        mesh=fine,
        in_specs=placed,
        out_specs=(P(seq, head, None), P(seq + head, None)),
        check_vma=False,
    )
```

```python
import functools

import jax
import jax.numpy as jnp
import numpy as np
from jax import lax
from jax.experimental import pallas as pl
from jax.experimental.pallas import tpu as pltpu
from jax.sharding import Mesh
from jax.sharding import PartitionSpec as P

H_LOC = 4
DL = 512
DR = 64
DK = 576
TILE = 256
HALF = 128
NG = 8
KEYS = NG * TILE
LOG2E = 1.4426950408889634
FLOOR = -1e30
LANES = 128
OWNED = 32
PACKED = OWNED * DK // LANES
MAIN_VMEM = 19 * 1024 * 1024
FIRST = 3

softmax_scale = 0.07216878364870322

BF = jnp.bfloat16
F32 = jnp.float32


def dot(a, b):
    return lax.dot_general(a, b, (((1,), (0,)), ((), ())), preferred_element_type=F32)


def dot_nt(a, b):
    return lax.dot_general(a, b, (((1,), (1,)), ((), ())), preferred_element_type=F32)


def directions(place_ref):
    core, zl = place_ref[0], place_ref[2]
    turn = 2 * core
    ahead = [(0 - dy) & 3 for dy in (0, 1 + turn, 1 + turn, 3 - turn, 3 - turn, 0, 2, 2)]
    floors = [zl ^ dz for dz in (0, 0, 1, 0, 1, 1, 0, 1)]
    return ahead, floors


def positions(place_ref, query_blocks_ref, key_blocks_ref):
    core, y, zl = (place_ref[n] for n in range(3))
    ahead, floors = directions(place_ref)
    mine = query_blocks_ref[y * 2 + zl]
    limits = []
    for up, floor in zip(ahead, floors):
        lag = (mine - key_blocks_ref[((y + up) & 3) * 2 + floor]) * TILE
        limits.append((lag - core * 8, lag - (core ^ 1) * 8))
    return limits


def halves(refs):
    return [[ref[...] for ref in refs[2 * n : 2 * n + 2]] for n in range(len(refs) // 2)]


def offsets():
    t = lax.broadcasted_iota(jnp.int32, (HALF, TILE), 0)
    i = lax.broadcasted_iota(jnp.int32, (HALF, TILE), 1)
    return (t >> 3) * 16 + (t & 7) - i


def span(c):
    return slice(c * TILE, (c + 1) * TILE)


def weigh(keys, qt, got, delta, limits):
    scores = dot(keys, qt) * (softmax_scale * LOG2E)
    parts = [
        jnp.where(delta <= limits[b], scores[b * HALF : (b + 1) * HALF], -jnp.inf)
        for b in range(2)
    ]
    peak = jnp.maximum(*[jnp.max(p, axis=0, keepdims=True) for p in parts])
    floor = jnp.maximum(peak, FLOOR)
    e = [jnp.exp2(p - floor) for p in parts]
    total = sum(jnp.sum(p, axis=0, keepdims=True) for p in e)
    return e, dot(keys[:, :DL], got), peak, total


def first_kernel(place_ref, query_blocks_ref, key_blocks_ref, qt_ref, go_ref, *refs):
    e_ref, gp_ref, stat_ref, gl_ref, gr_ref, got_ref, k_s = refs[2 * FIRST :]
    limits = positions(place_ref, query_blocks_ref, key_blocks_ref)
    for slot, pair in enumerate(halves(refs[: 2 * FIRST])):
        for b in range(2):
            at = slot * TILE + b * HALF
            k_s[at : at + HALF, :] = pair[b].T
    delta = offsets()
    for h in range(H_LOC):
        go = go_ref[h]
        gl_ref[h * 2 * TILE : h * 2 * TILE + TILE, :] = go
        got_ref[h] = go.T
        q = qt_ref[h].T
        gl_ref[h * 2 * TILE + TILE : (h + 1) * 2 * TILE, :] = q[:, :DL]
        gr_ref[h * TILE : (h + 1) * TILE, :] = q[:, DL:]
        for c in range(FIRST):
            e, gp, peak, total = weigh(k_s[span(c), :], qt_ref[h], got_ref[h], delta, limits[c])
            for b in range(2):
                at = c * TILE + b * HALF
                e_ref[h, at : at + HALF, :] = e[b]
            gp_ref[h, span(c), :] = gp
            stat_ref[0, h, c : c + 1, :] = peak
            stat_ref[1, h, c : c + 1, :] = total


def to_keys(place_ref, half, w_ref, gl_ref, gr_ref, ref):
    ahead, floors = directions(place_ref)
    core, x = place_ref[0], place_ref[3]
    later = core ^ half
    for c in range(NG // 2):
        w = w_ref[span(c), :]
        lat = dot(w, gl_ref[...])
        wr = jnp.concatenate(
            [w[:, (2 * h + 1) * TILE : (2 * h + 2) * TILE] for h in range(H_LOC)], axis=1
        )
        rope = dot(wr, gr_ref[...])
        for b in range(2):
            slot = 2 * c + b
            for to in range(4):
                at = b * HALF + to * OWNED
                right = (to - x) & 3
                i = jnp.where(later == 0, right, ahead[slot])
                j = jnp.where(later == 0, ahead[slot], right)
                for n in range(DL // LANES):
                    ref[i, j, floors[slot], n * OWNED : (n + 1) * OWNED, :] = lat[
                        at : at + OWNED, n * LANES : (n + 1) * LANES
                    ].astype(ref.dtype)
                both = jnp.concatenate(
                    [rope[at : at + OWNED // 2], rope[at + OWNED // 2 : at + OWNED]], axis=1
                )
                ref[i, j, floors[slot], DL // LANES * OWNED :, :] = both.astype(ref.dtype)


def main_kernel(place_ref, query_blocks_ref, key_blocks_ref, qt_ref, *refs):
    k_refs, refs = refs[: 2 * NG], refs[2 * NG :]
    e1_ref, gp1_ref, stat_ref, gl_ref, gr_ref, got_ref = refs[:6]
    own_w_ref, other_w_s, other_ref, kt_s, k_s, e_s, gp_s = refs[6:]
    limits = positions(place_ref, query_blocks_ref, key_blocks_ref)
    w_refs = (own_w_ref, other_w_s)
    for slot, pair in enumerate(halves(k_refs)):
        for b in range(2):
            at = b * KEYS // 2 + slot * HALF
            kt_s[:, at : at + HALF] = pair[b]
            if slot >= FIRST:
                at = (slot - FIRST) * TILE + b * HALF
                k_s[at : at + HALF, :] = pair[b].T
    delta = offsets()
    peaks = [[stat_ref[0, h, c : c + 1, :] for c in range(FIRST)] for h in range(H_LOC)]
    sums = [[stat_ref[1, h, c : c + 1, :] for c in range(FIRST)] for h in range(H_LOC)]
    factors = [None] * H_LOC
    corrs = [None] * H_LOC

    def load(h, c):
        if c < FIRST:
            return e1_ref[h, span(c), :], gp1_ref[h, span(c), :]
        return e_s[h, span(c - FIRST), :], gp_s[h, span(c - FIRST), :]

    def keep(h, c, kind, value):
        at = (2 * h + kind) * TILE
        for b, ref in enumerate(w_refs):
            ref[c * HALF : (c + 1) * HALF, at : at + TILE] = value[b * HALF : (b + 1) * HALF]

    def settle(h):
        peak = functools.reduce(jnp.maximum, peaks[h])
        shares = [jnp.exp2(p - peak) for p in peaks[h]]
        inv = 1.0 / sum(f * s for f, s in zip(shares, sums[h]))
        factors[h] = [f * inv for f in shares]
        corrs[h] = jnp.zeros((1, TILE), F32)

    def correct(h, c):
        e, gp = load(h, c)
        pb = (e * factors[h][c]).astype(BF)
        keep(h, c, 0, pb)
        corrs[h] = corrs[h] + jnp.sum(pb.astype(F32) * gp, axis=0, keepdims=True)

    def differ(h, c):
        e, gp = load(h, c)
        ds = (e * (factors[h][c] * softmax_scale) * (gp - corrs[h])).astype(BF)
        keep(h, c, 1, ds)

    for step in range(H_LOC + 2):
        if 1 <= step <= H_LOC:
            settle(step - 1)
        for c in range(NG):
            if step < H_LOC and c >= FIRST:
                e, gp, peak, total = weigh(
                    k_s[span(c - FIRST), :], qt_ref[step], got_ref[step], delta, limits[c]
                )
                for b in range(2):
                    at = (c - FIRST) * TILE + b * HALF
                    e_s[step, at : at + HALF, :] = e[b]
                gp_s[step, span(c - FIRST), :] = gp
                peaks[step].append(peak)
                sums[step].append(total)
            if 1 <= step <= H_LOC:
                correct(step - 1, c)
            if step >= 2:
                differ(step - 2, c)
    to_keys(place_ref, 1, other_w_s, gl_ref, gr_ref, other_ref)


def query_kernel(own_w_ref, other_w_ref, kt_ref, dqt_ref):
    for h in range(H_LOC):
        at = (2 * h + 1) * TILE
        for r in range(2):
            rows = slice(r * DK // 2, (r + 1) * DK // 2)
            out = dot(kt_ref[rows, : KEYS // 2], own_w_ref[:, at : at + TILE])
            out = out + dot(kt_ref[rows, KEYS // 2 :], other_w_ref[:, at : at + TILE])
            dqt_ref[h, rows, :] = out.astype(BF)


def own_kernel(place_ref, w_ref, gl_ref, gr_ref, own_ref):
    to_keys(place_ref, 0, w_ref, gl_ref, gr_ref, own_ref)


VMEM = pl.BlockSpec(memory_space=pltpu.VMEM)
SMEM = pl.BlockSpec(memory_space=pltpu.SMEM)


def first_part(place, query_blocks, key_blocks, qt, go, k_blocks):
    shapes = [
        ((H_LOC, FIRST * TILE, TILE), F32),
        ((H_LOC, FIRST * TILE, TILE), F32),
        ((2, H_LOC, 8, TILE), F32),
        ((H_LOC * 2 * TILE, DL), BF),
        ((H_LOC * TILE, DR), BF),
        ((H_LOC, DL, TILE), BF),
    ]
    return pl.pallas_call(
        first_kernel,
        in_specs=[SMEM] * 3 + [VMEM] * (2 + 2 * FIRST),
        out_specs=[VMEM] * len(shapes),
        out_shape=[jax.ShapeDtypeStruct(*s) for s in shapes],
        scratch_shapes=[pltpu.VMEM((FIRST * TILE, DK), BF)],
        cost_estimate=pl.CostEstimate(
            flops=2 * 1024 * FIRST * TILE * (DK + DL), bytes_accessed=20_000_000, transcendentals=0
        ),
        compiler_params=pltpu.CompilerParams(vmem_limit_bytes=16 * 1024 * 1024),
    )(place, query_blocks, key_blocks, qt, go, *k_blocks)


def main_part(place, query_blocks, key_blocks, qt, k_blocks, early):
    rest = (NG - FIRST) * TILE
    return pl.pallas_call(
        main_kernel,
        in_specs=[SMEM] * 3 + [VMEM] * (1 + len(k_blocks) + len(early)),
        out_specs=[VMEM] * 4,
        out_shape=[
            jax.ShapeDtypeStruct((KEYS // 2, H_LOC * 2 * TILE), BF),
            jax.ShapeDtypeStruct((KEYS // 2, H_LOC * 2 * TILE), BF),
            jax.ShapeDtypeStruct((4, 4, 2, PACKED, LANES), BF),
            jax.ShapeDtypeStruct((DK, KEYS), BF),
        ],
        scratch_shapes=[
            pltpu.VMEM((rest, DK), BF),
            pltpu.VMEM((H_LOC, rest, TILE), F32),
            pltpu.VMEM((H_LOC, rest, TILE), F32),
        ],
        compiler_params=pltpu.CompilerParams(vmem_limit_bytes=MAIN_VMEM),
    )(place, query_blocks, key_blocks, qt, *k_blocks, *early)


def query_part(own_weights, other_weights, kt):
    return pl.pallas_call(
        query_kernel,
        in_specs=[VMEM] * 3,
        out_specs=VMEM,
        out_shape=jax.ShapeDtypeStruct((H_LOC, DK, TILE), BF),
        cost_estimate=pl.CostEstimate(
            flops=2 * KEYS * H_LOC * TILE * DK, bytes_accessed=12_000_000, transcendentals=0
        ),
        compiler_params=pltpu.CompilerParams(vmem_limit_bytes=16 * 1024 * 1024),
    )(own_weights, other_weights, kt)


def own_part(place, weights, gl, gr):
    return pl.pallas_call(
        own_kernel,
        in_specs=[SMEM] + [VMEM] * 3,
        out_specs=VMEM,
        out_shape=jax.ShapeDtypeStruct((4, 4, 2, PACKED, LANES), F32),
        cost_estimate=pl.CostEstimate(
            flops=KEYS * H_LOC * 2 * TILE * DK, bytes_accessed=9_000_000, transcendentals=0
        ),
        compiler_params=pltpu.CompilerParams(vmem_limit_bytes=12 * 1024 * 1024),
    )(place, weights, gl, gr)


def swap_cores(x):
    return lax.ppermute(x, "c", [(0, 1), (1, 0)])


def onward(x, dz):
    pairs = [
        ((y * 2 + z) * 2 + c, ((y + 1 - 2 * c) % 4 * 2 + (z ^ dz)) * 2 + c)
        for y in range(4)
        for z in range(2)
        for c in range(2)
    ]
    return lax.ppermute(x, ("y", "zl", "c"), pairs)


def crossed(x, first, step):
    def target(n):
        y, x, c = n // 8, n // 2 % 4, n % 2
        if (c == 0) == first:
            x = (x + step) % 4
        else:
            y = (y + step) % 4
        return (y * 4 + x) * 2 + c

    return lax.ppermute(x, ("y", "x", "c"), [(n, target(n)) for n in range(32)])


def unpack(x):
    lat = x[: DL // LANES * OWNED].reshape(DL // LANES, 4, 8, LANES)
    lat = lat.transpose(1, 2, 0, 3).reshape(4, 8, DL)
    rope = x[DL // LANES * OWNED :].reshape(2, 8, 2, DR).transpose(2, 0, 1, 3).reshape(4, 8, DR)
    return jnp.concatenate([lat, rope], axis=2)


def shards(queries, latent_cache, grad_output, query_blocks, key_blocks):
    core, y, zl, x = (lax.axis_index(a) for a in ("c", "y", "zl", "x"))
    row = lax.broadcasted_iota(jnp.int32, (TILE, TILE), 0)
    t = lax.broadcasted_iota(jnp.int32, (TILE, TILE), 1)
    half, t = t >> 7, t & 127
    pick = (row == (t >> 3) * 16 + (core ^ half) * 8 + (t & 7)).astype(BF)
    here = lax.dot_general(
        latent_cache, pick, (((0,), (0,)), ((), ())), preferred_element_type=F32
    ).astype(BF)
    mine, rest = here[:, :HALF], here[:, HALF:]

    slant = [onward(mine, 1)]
    near = [onward(mine, 0)]
    beside = lax.ppermute(mine, "zl", [(0, 1), (1, 0)])
    slant.append(onward(rest, 1))
    near.append(onward(rest, 0))
    place = jnp.stack([core, y, zl, x])

    qt = queries.transpose(1, 2, 0)
    go = grad_output.transpose(1, 0, 2)
    far = [onward(near[0], 0), onward(slant[0], 0)]
    blocks = [mine, rest] + near + slant
    early = list(first_part(place, query_blocks, key_blocks, qt, go, blocks))
    early[2], beside, *whole = lax.optimization_barrier((early[2], beside, *near, *slant))
    for pair in (whole[:2], whole[2:]):
        blocks += [swap_cores(pair[1]), swap_cores(pair[0])]
    early[2], *far = lax.optimization_barrier((early[2], *far))
    for k in [beside] + far:
        blocks += [k, swap_cores(k)]
    weights, other_weights, other, kt = main_part(place, query_blocks, key_blocks, qt, blocks, early)
    other = swap_cores(other)
    own = own_part(place, weights, early[3], early[4])

    sums = [own[d] + other[d].astype(F32) for d in range(4)]
    kt, *sums = lax.optimization_barrier((kt, *sums))
    dqt = query_part(weights, other_weights, kt)
    for first in (True, False):
        got = [crossed(sums[d].astype(BF), first, d) for d in (2, 1, 3)]
        if first:
            dqt, *got = lax.optimization_barrier((dqt, *got))
        sums = sums[0] + sum(g.astype(F32) for g in got)
    part = jnp.concatenate([unpack(sums[z]).astype(BF) for z in range(2)], axis=0)
    got = lax.all_to_all(part, ("zl", "zh"), 0, 0, tiled=True)
    return dqt.transpose(2, 0, 1), jnp.sum(got.astype(F32), axis=0)


def solution(mesh):
    fine = Mesh(mesh.devices.reshape(4, 2, 4, 4, 2), ("y", "zl", "x", "zh", "c"))
    seq, head = ("y", "zl"), ("x", "zh", "c")
    placed = (P(seq, head, None), P(seq, None), P(seq, head, None), P(), P())
    return jax.shard_map(
        shards,
        mesh=fine,
        in_specs=placed,
        out_specs=(P(seq, head, None), P(seq + head, None)),
        check_vma=False,
    )
```
